32 devices in a mesh: tests: 8 (over z, x), branches: 4 (over y, core).
Axes of the slice: x: 2, y: 2, z: 4, core: 2. Of those that a mesh axis runs over, the one named last changes fastest.
Arguments:
- select: float32 [131072], P('tests'), may hold values from 1e-05 to 0.95
- tiles: float32 [2048, 128, 128], P(('tests', 'branches')), may hold values from 0.0001 to 0.9
- row_block: int32 [2048], P(('tests', 'branches')), may hold values from 0 to 127
- col_block: int32 [2048], P(('tests', 'branches')), may hold values from 0 to 2047, as said below
- counts: int32 [32], P(('tests', 'branches')), may hold values from 1 to 64, 1280 in all
- weights: float32 [1048576], P('branches'), may hold values from 1 to 16
Outputs:
- grad_tests: float32 [131072], P('tests')
- tile_grads: float32 [2048, 128, 128], P(('tests', 'branches'))
- next_select: float32 [131072], P('tests')
The draws below stay inside these ranges and needn't reach their ends.
Inputs may be any that keep to these rules, and one draw needn't show every extreme that they name: counts[d] is the number of device d's slots, from its first, that hold tiles. Call col_block[s] // 256 the share of slot s. Of the 64 slots of one device at most 12 have one share; in every index of branches one share holds exactly 12 slots of every device there.
All inputs are finite; a program needn't handle non-finite values.
Results may differ from the reference program's by a relative error of at most 0.0003.
Values sent between devices are 32-bit elements; how exact they have to be, the bound alone decides.
No kernel may reach another device: no remote copies, remote signals or barrier semaphores. Data moves between devices by JAX's collectives and lax.ppermute only.
A program may use at most 64 MiB of HBM per device.

```python
import math
import jax
import jax.numpy as jnp
import numpy as np
from jax import lax

TILE = 128
CAP = 64
TB_DEV = 128
BB_DEV = 2048
STEPS = 2
TESTS = 131072
BRANCHES = 1048576
SLOTS = 2048
FILLED = 1280
ROUTE = 12
N_TESTS = 8
N_BRANCHES = 4


def draw_col_block(key, part):
    key = jax.random.fold_in(key, 7)
    devices = N_TESTS * N_BRANCHES
    share = BB_DEV // N_TESTS
    seats = (N_TESTS - 1) * ROUTE
    rest = CAP - ROUTE
    full_owner = jax.random.randint(jax.random.fold_in(key, 1), (N_BRANCHES,), 0, N_TESTS).astype(jnp.int32)
    device_full = jnp.tile(full_owner, N_TESTS)
    scores = jax.random.randint(jax.random.fold_in(key, 2), (devices, seats), 0, 1 << 15).astype(jnp.int32)
    scores = scores * seats + jnp.arange(seats, dtype=jnp.int32)[None, :]
    order = jnp.argsort(scores, axis=1, stable=True)[:, :rest].astype(jnp.int32)
    other_rank = order // ROUTE
    others = other_rank + (other_rank >= device_full[:, None]).astype(jnp.int32)
    offset = jax.random.randint(jax.random.fold_in(key, 3), (devices,), 0, rest + 1).astype(jnp.int32)
    position = jnp.arange(CAP, dtype=jnp.int32)[None, :]
    in_group = (position >= offset[:, None]) & (position < offset[:, None] + ROUTE)
    index = jnp.where(position < offset[:, None], position, position - ROUTE)
    index = jnp.clip(index, 0, rest - 1).astype(jnp.int32)
    picked = jnp.take_along_axis(others, index, axis=1)
    owners = jnp.where(in_group, device_full[:, None], picked)
    inside = jax.random.randint(jax.random.fold_in(key, 4), (devices, CAP), 0, share).astype(jnp.int32)
    return (owners * share + inside).reshape(-1).astype(jnp.int32)


def plant(drawn, key, smallest, high):
    longest = drawn.shape.index(max(drawn.shape))
    spots = []
    for shift in (0, 1):
        where = [jax.random.randint(jax.random.fold_in(key, axis), (), 0, length) for axis, length in enumerate(drawn.shape)]
        where[longest] = (where[longest] + shift) % drawn.shape[longest]
        spots.append(tuple(where))
    return drawn.at[spots[0]].set(smallest).at[spots[1]].set(high)


def block_levels(key, extent, shards, low, top_value):
    factor_of, own = 1.0, jax.random.fold_in(key, 6)
    for dim, shards_of in shards:
        steps = jnp.exp(jax.random.uniform(jax.random.fold_in(own, dim), (shards_of,), jnp.float32, low / len(shards), top_value / len(shards)))
        factor_of = factor_of * jnp.repeat(steps, extent[dim] // shards_of).reshape([-1 if axis == dim else 1 for axis in range(len(extent))])
    return factor_of


def split_up(count, total, reach, slope):
    loads = [(1 << 20) // math.isqrt(rank ** slope) + 1 for rank in range(2, count + 1)]
    spare, holding = total - reach - (count - 1), [1] * (count - 1)
    while spare > 0:
        free = [i for i in range(count - 1) if holding[i] < reach]
        whole, budget = sum([loads[i] for i in free]), spare
        for i in free:
            more = min(reach - holding[i], max(1, budget * loads[i] // whole), spare)
            holding[i] = holding[i] + more
            spare = spare - more
    return np.array([reach] + holding)


def uneven_parts(stream_key, count, total, limit, lean):
    if count == 2:
        one = jax.random.randint(stream_key, (), max(1, total - limit), min(limit, total - 1) + 1)
        return jnp.stack([one, total - one])
    sizes = jnp.asarray(split_up(count, total, limit, lean), jnp.int32)
    pairs = (count - 1) // 2
    giver, taker = sizes[1:1 + 2 * pairs:2], sizes[2:2 + 2 * pairs:2]
    slack = jnp.minimum(giver - 1, limit - taker)
    moved = jax.random.randint(jax.random.fold_in(stream_key, 1), (pairs,), 0, 1 << 20) % (slack + 1)
    sizes = sizes.at[1:1 + 2 * pairs:2].set(giver - moved).at[2:2 + 2 * pairs:2].set(taker + moved)
    return sizes[jax.random.permutation(jax.random.fold_in(stream_key, 2), count)]


def setup_inputs(seed: int = 0) -> dict:
    seeds = jax.random.split(jax.random.key(seed), 7)
    select = jnp.clip(jnp.exp(math.log(0.95) - 11.461632 * jax.random.uniform(seeds[0], (TESTS,), jnp.float32) ** block_levels(seeds[0], (TESTS,), ((0, 8),), -0.2, 0.2)), 9.999999747378752e-06, 0.95)
    tiles = jnp.clip(jnp.exp(math.log(0.9) - 9.1049799 * jax.random.uniform(seeds[1], (SLOTS, TILE, TILE), jnp.float32) ** block_levels(seeds[1], (SLOTS, TILE, TILE), ((0, 32),), -0.2, 0.2)), 0.0001, 0.9)
    row_block = plant(jax.random.randint(seeds[2], (SLOTS,), 0, TB_DEV), jax.random.fold_in(seeds[2], 1), 0, TB_DEV - 1).astype(jnp.int32)
    col_block = draw_col_block(jax.random.fold_in(seeds[6], 71), 0)
    counts = uneven_parts(seeds[4], N_TESTS * N_BRANCHES, FILLED, CAP, 2).astype(jnp.int32)
    weights = jnp.clip(jnp.exp(math.log(16.0) - 2.7725887 * jax.random.uniform(seeds[5], (BRANCHES,), jnp.float32) ** block_levels(seeds[5], (BRANCHES,), ((0, 4),), -0.2, 0.2)), 1.0, 16.0)
    return dict(select=select, tiles=tiles, row_block=row_block, col_block=col_block, counts=counts, weights=weights)


ascent_rate = 0.0015
select_cap = 0.5


def device_layout(device, row_block, col_block, counts):
    start = device * CAP
    rows = lax.dynamic_slice_in_dim(row_block, start, CAP) + (device // N_BRANCHES) * TB_DEV
    columns = lax.dynamic_slice_in_dim(col_block, start, CAP) + (device % N_BRANCHES) * BB_DEV
    live = jnp.arange(CAP, dtype=jnp.int32) < counts[device]
    return start, rows.astype(jnp.int32), columns.astype(jnp.int32), live


def log_survival(current, tiles, row_block, col_block, counts):
    blocks = current.reshape(TB_DEV * N_TESTS, TILE)

    def visit(total, device):
        start, rows, columns, live = device_layout(device, row_block, col_block, counts)
        piece = lax.dynamic_slice_in_dim(tiles, start, CAP)
        picked = blocks[rows]
        logs = jnp.sum(jnp.log1p(-picked[:, :, None] * piece), axis=1)
        logs = jnp.where(live[:, None], logs, jnp.zeros_like(logs))
        return total.at[columns].add(logs), None

    zero = jnp.zeros((BB_DEV * N_BRANCHES, TILE), jnp.float32)
    total, _ = lax.scan(visit, zero, jnp.arange(N_TESTS * N_BRANCHES, dtype=jnp.int32))
    return total


def gradients(current, survival, tiles, row_block, col_block, counts, keep_tiles):
    blocks = current.reshape(TB_DEV * N_TESTS, TILE)

    def visit(total, device):
        start, rows, columns, live = device_layout(device, row_block, col_block, counts)
        piece = lax.dynamic_slice_in_dim(tiles, start, CAP)
        picked = blocks[rows]
        inverse = 1.0 / (1.0 - picked[:, :, None] * piece)
        scaled = survival[columns][:, None, :] * inverse
        terms = jnp.sum(scaled * piece, axis=2)
        terms = jnp.where(live[:, None], terms, jnp.zeros_like(terms))
        total = total.at[rows].add(terms)
        if keep_tiles:
            tile_part = scaled * picked[:, :, None]
            tile_part = jnp.where(live[:, None, None], tile_part, jnp.zeros_like(tile_part))
            return total, tile_part
        return total, None

    zero = jnp.zeros((TB_DEV * N_TESTS, TILE), jnp.float32)
    total, tile_parts = lax.scan(visit, zero, jnp.arange(N_TESTS * N_BRANCHES, dtype=jnp.int32))
    return total.reshape(-1), tile_parts


def reference(select, tiles, row_block, col_block, counts, weights):
    current = select
    weight_rows = weights.reshape(BB_DEV * N_BRANCHES, TILE)
    grad_tests = current
    tile_grads = tiles
    for step in range(STEPS):
        keep = step == STEPS - 1
        summed = log_survival(current, tiles, row_block, col_block, counts)
        survival = weight_rows * jnp.exp(summed)
        gradient, tile_parts = gradients(current, survival, tiles, row_block, col_block, counts, keep)
        if keep:
            grad_tests = gradient
            tile_grads = tile_parts.reshape(SLOTS, TILE, TILE)
        rate = ascent_rate * gradient
        current = current + (select_cap - current) * rate / (1.0 + rate)
    return grad_tests, tile_grads, current
```

```python
import functools

import jax
import jax.numpy as jnp
from jax import lax
from jax.experimental import pallas as pl
from jax.experimental.pallas import tpu as pltpu
from jax.sharding import PartitionSpec as P

STEPS = 2
GROUP = 8
EXTRA = 8
F32 = jnp.float32
BF16 = jnp.bfloat16

ascent_rate = 0.0015
select_cap = 0.5


def pieces(x):
    high = x.astype(BF16)
    rest = x - high.astype(F32)
    middle = rest.astype(BF16)
    low = (rest - middle.astype(F32)).astype(BF16)
    return high, middle, low


def pick(ones, x):
    total = jnp.zeros((ones.shape[0], x.shape[1]), F32)
    for piece in pieces(x)[::-1]:
        total = total + jnp.dot(ones, piece, preferred_element_type=F32)
    return total


def inverse_of(x):
    guess = pl.reciprocal(x, approx=True)
    return guess * (2.0 - x * guess)


def spread(values, count, width, fill):
    rows = [jnp.full((1, width), values[s], jnp.int32) for s in range(count)]
    rows.append(jnp.full((width - count, width), fill, jnp.int32))
    return jnp.concatenate(rows, axis=0)


def pick_columns(rows, blocks, picked, columns):
    slots = rows.shape[0]
    for s in range(slots):
        picked[pl.ds(s, 1), :] = blocks[pl.ds(rows[s], 1), :]
    columns[...] = picked[...].T


def shifted(columns, group):
    width = columns.shape[1]
    return pltpu.roll(columns[...], lax.rem(width - group * GROUP, width), 1)


def slot_pass(group, limit, columns, tiles, ratios, logs):
    now = shifted(columns, group)
    for i in range(GROUP):
        s = group * GROUP + i
        tile = tiles[s]
        left = 1.0 - now[:, i : i + 1] * tile
        ratios[s] = tile * inverse_of(left)
        product = left[:8]
        for at in range(8, left.shape[0], 8):
            product = product * left[at : at + 8]
        row = jnp.sum(jnp.log(product), axis=0, keepdims=True)
        logs[pl.ds(s, 1), :] = jnp.where(s < limit, row, jnp.zeros_like(row))


def first_kernel(limit, rows, cols, blocks, tiles, weights, payload, ratios, held, slot_weights, picked, columns, tile_sem, weight_sem):
    slots, width = held.shape[0], held.shape[1]
    groups = slots // GROUP

    def tile_copy(group):
        part = pl.ds(group * GROUP, GROUP)
        return pltpu.make_async_copy(tiles.at[part], held.at[part], tile_sem.at[group])

    def weight_copy(s):
        return pltpu.make_async_copy(weights.at[pl.ds(cols[s], 1)], slot_weights.at[pl.ds(s, 1)], weight_sem)

    for group in range(groups):
        tile_copy(group).start()
    for s in range(slots):
        weight_copy(s).start()
    picked[...] = jnp.zeros_like(picked)
    pick_columns(rows, blocks, picked, columns)
    payload[pl.ds(slots, EXTRA), :] = spread(cols, slots, width, -1).T[:EXTRA].astype(F32)

    def step(group, carry):
        tile_copy(group).wait()
        slot_pass(group, limit[0], columns, held, ratios, payload)
        return carry

    lax.fori_loop(0, groups, step, 0)
    pltpu.make_async_copy(weights.at[pl.ds(0, slots)], slot_weights, weight_sem).wait()


def survive(limit, cols, gathered, others, slot_weights):
    slots, width = slot_weights.shape
    mine = jnp.concatenate([jnp.full((1, width), cols[s], jnp.int32) for s in range(slots)], axis=0).astype(F32)
    total = jnp.zeros((slots, width), F32)
    for j in range(gathered.shape[0]):
        same = jnp.where(mine == others[j, pl.ds(slots, 1), :], 1.0, 0.0).astype(BF16)
        total = total + pick(same[:, :slots], gathered[j, pl.ds(0, slots), :])
    live = lax.broadcasted_iota(jnp.int32, (slots, width), 0) < limit[0]
    return jnp.where(live, slot_weights[...] * jnp.exp(total), 0.0)


def tests_sums(rows, survival, ratios):
    slots, width = survival.shape
    lanes = lax.broadcasted_iota(jnp.int32, (width, width), 1)

    def step(group, total):
        for i in range(GROUP):
            s = group * GROUP + i
            terms = jnp.sum(ratios[s] * survival[pl.ds(s, 1), :], axis=1, keepdims=True)
            total = jnp.where(lanes == s, terms, total)
        return total

    sums = lax.fori_loop(0, slots // GROUP, step, jnp.zeros((width, width), F32)).T
    targets = spread(rows, slots, width, -1).T
    hits = jnp.where(targets == lax.broadcasted_iota(jnp.int32, (width, width), 0), 1.0, 0.0).astype(BF16)
    return pick(hits, sums)


def gradient_kernel(limit, rows, cols, gathered, others, slot_weights, ratios, partial, survival):
    survival[...] = survive(limit, cols, gathered, others, slot_weights)
    partial[...] = tests_sums(rows, survival, ratios)


def advance(current, gradient):
    rate = ascent_rate * gradient
    return current + (select_cap - current) * rate / (1.0 + rate)


def total_of(parts):
    while len(parts) > 1:
        parts = [a + b for a, b in zip(parts[::2], parts[1::2])]
    return parts[0]


def next_kernel(limit, rows, blocks, held, *refs):
    *partials, current, logs, ratios, picked, columns = refs
    current[...] = advance(blocks[...], total_of([p[...] for p in partials]))
    picked[...] = jnp.zeros_like(picked)
    pick_columns(rows, current, picked, columns)

    def step(group, carry):
        slot_pass(group, limit[0], columns, held, ratios, logs)
        return carry

    lax.fori_loop(0, held.shape[0] // GROUP, step, 0)


def tile_kernel(rows, blocks, survival, held, out, picked, columns):
    group = pl.program_id(0)

    @pl.when(group == 0)
    def _():
        picked[...] = jnp.zeros_like(picked)
        pick_columns(rows, blocks, picked, columns)

    now = shifted(columns, group)
    for i in range(GROUP):
        s = group * GROUP + i
        share = now[:, i : i + 1]
        out[i] = survival[pl.ds(s, 1), :] * share * inverse_of(1.0 - share * held[s])


SMEM = pl.BlockSpec(memory_space=pltpu.SMEM)
VMEM = pl.BlockSpec(memory_space=pltpu.VMEM)
ANY = pl.BlockSpec(memory_space=pl.ANY)
PARAMS = pltpu.CompilerParams(vmem_limit_bytes=24 << 20)


def body(tests, branches, select, tiles, row_block, col_block, counts, weights):
    slots, width = tiles.shape[0], tiles.shape[1]
    blocks = select.reshape(-1, width)
    weight_rows = weights.reshape(-1, width)
    test_rows = blocks.shape[0]
    square = pltpu.VMEM((width, width), F32)
    full = jax.ShapeDtypeStruct(tiles.shape, F32)
    per_slot = jax.ShapeDtypeStruct((slots, width), F32)
    per_test = jax.ShapeDtypeStruct((test_rows, width), F32)

    def over_tests(x):
        return lax.all_to_all(jnp.broadcast_to(x[None], (tests,) + x.shape), "tests", 0, 0)

    def over_branches(x):
        return [x] + [lax.ppermute(x, "branches", [(b, b ^ k) for b in range(branches)]) for k in range(1, branches)]

    payload, ratios, held, slot_weights = pl.pallas_call(
        first_kernel,
        out_shape=(jax.ShapeDtypeStruct((slots + EXTRA, width), F32), full, full, per_slot),
        in_specs=[SMEM, SMEM, SMEM, VMEM, ANY, ANY],
        out_specs=(VMEM,) * 4,
        scratch_shapes=[square, square, pltpu.SemaphoreType.DMA((slots // GROUP,)), pltpu.SemaphoreType.DMA],
        compiler_params=PARAMS,
        name="first_logs",
    )(counts, row_block, col_block, blocks, tiles, weight_rows)
    others = over_tests(payload)
    gathered = others
    current = blocks
    for step in range(STEPS):
        partial, survival = pl.pallas_call(
            gradient_kernel,
            out_shape=(per_test, per_slot),
            in_specs=[SMEM, SMEM, SMEM, VMEM, VMEM, VMEM, VMEM],
            out_specs=(VMEM, VMEM),
            compiler_params=PARAMS,
            name="gradient",
        )(counts, row_block, col_block, gathered, others, slot_weights, ratios)
        partials = over_branches(partial)
        if step < STEPS - 1:
            current, logs, ratios = pl.pallas_call(
                next_kernel,
                out_shape=(per_test, per_slot, full),
                in_specs=[SMEM, SMEM, VMEM, VMEM] + [VMEM] * branches,
                out_specs=(VMEM,) * 3,
                scratch_shapes=[square, square],
                compiler_params=PARAMS,
                name="next_logs",
            )(counts, row_block, current, held, *partials)
            gathered = over_tests(logs)
    tile_grads = pl.pallas_call(
        tile_kernel,
        grid=(slots // GROUP,),
        out_shape=full,
        in_specs=[SMEM, VMEM, VMEM, VMEM],
        out_specs=pl.BlockSpec((GROUP, width, width), lambda i: (i, 0, 0)),
        scratch_shapes=[square, square],
        compiler_params=PARAMS,
        name="tile_gradients",
    )(row_block, current, survival, held)
    gradient = total_of(partials)
    return gradient.reshape(-1), tile_grads, advance(current, gradient).reshape(-1)


def solution(mesh):
    return jax.shard_map(
        functools.partial(body, mesh.shape["tests"], mesh.shape["branches"]),
        mesh=mesh,
        in_specs=(
            P("tests"),
            P(("tests", "branches"), None, None),
            P(("tests", "branches")),
            P(("tests", "branches")),
            P(("tests", "branches")),
            P("branches"),
        ),
        out_specs=(P("tests"), P(("tests", "branches"), None, None), P("tests")),
        check_vma=False,
    )
```

```python
import functools

import jax
import jax.numpy as jnp
from jax import lax
from jax.experimental import pallas as pl
from jax.experimental.pallas import tpu as pltpu
from jax.sharding import PartitionSpec as P

GROUP = 8
EXTRA = 8
CHUNK = 8
F32 = jnp.float32
BF16 = jnp.bfloat16

ascent_rate = 0.0015
select_cap = 0.5


def pieces(x):
    high = x.astype(BF16)
    rest = x - high.astype(F32)
    middle = rest.astype(BF16)
    low = (rest - middle.astype(F32)).astype(BF16)
    return high, middle, low


def pick(ones, x):
    width = x.shape[1]
    parts = jnp.dot(ones, jnp.concatenate(pieces(x), axis=1), preferred_element_type=F32)
    return parts[:, :width] + (parts[:, width : 2 * width] + parts[:, 2 * width :])


def inverse_of(x):
    guess = pltpu.reciprocal(x, approx=True)
    return guess * (2.0 - x * guess)


def hits_of(ids, test_rows):
    shape = (test_rows, ids.shape[1])
    return jnp.where(ids == lax.broadcasted_iota(jnp.int32, shape, 0).astype(F32), 1.0, 0.0).astype(BF16)


def columns_of(blocks, hits):
    return pick_rows(blocks.T, hits)


def pick_rows(x, ones):
    high, middle, low = [jnp.dot(piece, ones, preferred_element_type=F32) for piece in pieces(x)]
    return high + (middle + low)


def slot_pass(s, columns, tiles, ratios, logs):
    tile = tiles[s]
    left = 1.0 - columns[:, s : s + 1] * tile
    ratios[s] = tile * inverse_of(left)
    product = left[:8]
    for at in range(8, left.shape[0], 8):
        product = product * left[at : at + 8]
    logs[s : s + 1, :] = jnp.sum(jnp.log(product), axis=0, keepdims=True)


def first_kernel(limit, rows, cols, blocks, tiles, weights, payload, ratios, held, slot_weights, ids, mine, near, row_lanes, col_lanes, own, sems, tile_sem, weight_sem):
    slots, width = held.shape[0], held.shape[1]
    small = [
        pltpu.make_async_copy(source, target, sems.at[i])
        for i, (source, target) in enumerate(((cols, near), (cols, col_lanes), (rows, row_lanes), (blocks, own)))
    ]
    for copy in small:
        copy.start()
    tile_copies = []
    for group in range(slots // GROUP):
        part = pl.ds(group * GROUP, GROUP)
        tile_copies.append(pltpu.make_async_copy(tiles.at[part], held.at[part], tile_sem.at[group]))
        tile_copies[-1].start()
    small[0].wait()
    for s in range(slots):
        pltpu.make_async_copy(weights.at[pl.ds(near[0, s], 1)], slot_weights.at[pl.ds(s, 1)], weight_sem).start()
    for copy in small[1:]:
        copy.wait()
    live = lax.broadcasted_iota(jnp.int32, (1, slots), 1) < limit[0]
    lanes = jnp.where(live, col_lanes[...], -1).astype(F32)
    payload[slots:, :] = jnp.broadcast_to(jnp.concatenate([lanes] * (width // slots), axis=1), (EXTRA, width))
    mine[...] = jnp.broadcast_to(col_lanes[...].astype(F32), (width, slots)).T
    own_ids = row_lanes[...].astype(F32)
    ids[...] = jnp.broadcast_to(jnp.concatenate([own_ids] * (width // slots), axis=1), (EXTRA, width))
    columns = columns_of(own[...], hits_of(own_ids, own.shape[0]))
    for s in range(slots):
        if s % GROUP == 0:
            tile_copies[s // GROUP].wait()
        slot_pass(s, columns, held, ratios, payload)
    pltpu.make_async_copy(weights.at[pl.ds(0, slots)], slot_weights, weight_sem).wait()
    alive = lax.broadcasted_iota(jnp.int32, (slots, width), 0) < limit[0]
    slot_weights[...] = jnp.where(alive, slot_weights[...], 0.0)


def survive(gathered, others, mine, slot_weights):
    slots, width = slot_weights.shape
    here = mine[...]
    lanes = lax.broadcasted_iota(jnp.int32, (slots, width), 1)
    each = width // slots
    total = jnp.zeros((slots, width), F32)
    for start in range(0, gathered.shape[0], CHUNK):
        same = []
        for j in range(start, start + CHUNK, each):
            there = others[j, slots : slots + 1, :]
            for k in range(1, each):
                there = jnp.where(lanes < k * slots, there, others[j + k, slots : slots + 1, :])
            same.append(jnp.where(here == there, 1.0, 0.0).astype(BF16))
        rows = jnp.concatenate([gathered[j, :slots, :] for j in range(start, start + CHUNK)], axis=0)
        total = total + pick(jnp.concatenate(same, axis=1), rows)
    return slot_weights[...] * jnp.exp(total)


def slot_sums(survival, ratios, out):
    slots, width = survival.shape
    lanes = lax.broadcasted_iota(jnp.int32, (width, width), 1)
    ones = jnp.ones((width, width), BF16)
    total = jnp.zeros((width, width), F32)
    for s in range(slots):
        terms = ratios[s] * survival[s : s + 1, :]
        if s % 3 == 2:
            high = terms.astype(BF16)
            low = (terms - high.astype(F32)).astype(BF16)
            sums = jnp.dot(high, ones, preferred_element_type=F32) + jnp.dot(low, ones, preferred_element_type=F32)
        else:
            sums = jnp.sum(terms, axis=1, keepdims=True)
        total = jnp.where(lanes == s, sums, total)
    out[:slots, :] = total.T[:slots]


def gradient_kernel(gathered, mine, slot_weights, ratios, ids, out):
    slots = slot_weights.shape[0]
    slot_sums(survive(gathered, gathered, mine, slot_weights), ratios, out)
    out[slots:, :] = ids[...]


def last_gradient_kernel(gathered, others, mine, slot_weights, ratios, out, survival):
    survival[...] = survive(gathered, others, mine, slot_weights)
    slot_sums(survival[...], ratios, out)


def advance(current, gradient):
    rate = ascent_rate * gradient
    return current + (select_cap - current) * rate / (1.0 + rate)


def gradient_of(parts, ids, test_rows):
    slots = ids[0].shape[0] - EXTRA
    sums = [pick(hits_of(i[slots : slots + 1, :slots], test_rows), p[:slots, :]) for p, i in zip(parts, ids)]
    while len(sums) > 1:
        sums = [a + b for a, b in zip(sums[::2], sums[1::2])]
    return sums[0]


def next_kernel(blocks, held, *refs):
    *parts, current, logs, ratios = refs
    current[...] = advance(blocks[...], gradient_of(parts, parts, blocks.shape[0]))
    slots = held.shape[0]
    columns = columns_of(current[...], hits_of(parts[0][slots : slots + 1, :slots], blocks.shape[0]))
    for s in range(slots):
        slot_pass(s, columns, held, ratios, logs)


def tile_kernel(blocks, ids, survival, held, out, made, sems):
    slots = held.shape[0]
    columns = columns_of(blocks[...], hits_of(ids[:1, :slots], blocks.shape[0]))
    copies = []
    for s in range(slots):
        share = columns[:, s : s + 1]
        made[s] = survival[s : s + 1, :] * share * inverse_of(1.0 - share * held[s])
        if s % GROUP == GROUP - 1:
            part = pl.ds(s + 1 - GROUP, GROUP)
            copies.append(pltpu.make_async_copy(made.at[part], out.at[part], sems.at[s // GROUP]))
            copies[-1].start()
    for copy in copies:
        copy.wait()


def last_kernel(branches, current, *refs):
    *given, gradient, following = refs
    total = gradient_of(given[:branches], given[branches:], current.shape[0])
    gradient[...] = total
    following[...] = advance(current[...], total)


SMEM = pl.BlockSpec(memory_space=pltpu.SMEM)
VMEM = pl.BlockSpec(memory_space=pltpu.VMEM)
HBM = pl.BlockSpec(memory_space=pltpu.HBM)
PARAMS = pltpu.CompilerParams(vmem_limit_bytes=24 << 20)


def body(tests, branches, select, tiles, row_block, col_block, counts, weights):
    slots, width = tiles.shape[0], tiles.shape[1]
    blocks = select.reshape(-1, width)
    weight_rows = weights.reshape(-1, width)
    full = jax.ShapeDtypeStruct(tiles.shape, F32)
    per_slot = jax.ShapeDtypeStruct((slots, width), F32)
    labelled = jax.ShapeDtypeStruct((slots + EXTRA, width), F32)
    label = jax.ShapeDtypeStruct((EXTRA, width), F32)
    per_test = jax.ShapeDtypeStruct(blocks.shape, F32)
    lanes = pltpu.VMEM((1, slots), jnp.int32)
    dma = pltpu.SemaphoreType.DMA

    def call(kernel, outs, ins, name, **more):
        return pl.pallas_call(
            kernel,
            out_shape=outs,
            in_specs=more.pop("in_specs", [VMEM] * len(ins)),
            out_specs=more.pop("out_specs", jax.tree.map(lambda _: VMEM, outs)),
            compiler_params=PARAMS,
            name=name,
            **more,
        )(*ins)

    def over_tests(x):
        return lax.all_to_all(jnp.broadcast_to(x[None], (tests,) + x.shape), "tests", 0, 0)

    def over_branches(x):
        return [x] + [lax.ppermute(x, "branches", [(b, b ^ k) for b in range(branches)]) for k in range(1, branches)]

    payload, ratios, held, slot_weights, ids, mine = call(
        first_kernel,
        (labelled, full, full, per_slot, label, per_slot),
        (counts, row_block.reshape(1, -1), col_block.reshape(1, -1), blocks, tiles, weight_rows),
        "first_logs",
        in_specs=[SMEM] + [HBM] * 5,
        scratch_shapes=[
            pltpu.SMEM((1, slots), jnp.int32),
            lanes,
            lanes,
            pltpu.VMEM(blocks.shape, F32),
            dma((4,)),
            dma((slots // GROUP,)),
            dma,
        ],
    )
    others = over_tests(payload)
    parts = over_branches(call(gradient_kernel, labelled, (others, mine, slot_weights, ratios, ids), "gradient"))
    current, logs, ratios = call(next_kernel, (per_test, per_slot, full), (blocks, held, *parts), "next_logs")
    sums, survival = call(
        last_gradient_kernel, (per_slot, per_slot), (over_tests(logs), others, mine, slot_weights, ratios), "last_gradient"
    )
    last_parts = over_branches(sums)
    tile_grads = call(
        tile_kernel,
        full,
        (current, ids, survival, held),
        "tile_gradients",
        out_specs=HBM,
        scratch_shapes=[pltpu.VMEM(tiles.shape, F32), dma((slots // GROUP,))],
    )
    gradient, following = call(
        functools.partial(last_kernel, branches), (per_test, per_test), (current, *last_parts, *parts), "last_update"
    )
    return gradient.reshape(-1), tile_grads, following.reshape(-1)


def solution(mesh):
    return jax.shard_map(
        functools.partial(body, mesh.shape["tests"], mesh.shape["branches"]),
        mesh=mesh,
        in_specs=(
            P("tests"),
            P(("tests", "branches"), None, None),
            P(("tests", "branches")),
            P(("tests", "branches")),
            P(("tests", "branches")),
            P("branches"),
        ),
        out_specs=(P("tests"), P(("tests", "branches"), None, None), P("tests")),
        check_vma=False,
    )
```

```python
import functools

import jax
import jax.numpy as jnp
from jax import lax
from jax.experimental import pallas as pl
from jax.experimental.pallas import tpu as pltpu
from jax.sharding import PartitionSpec as P

GROUP = 8
EXTRA = 8
CHUNK = 8
FEW = 16
HALVES = 2
SHARED = 3
F32 = jnp.float32
BF16 = jnp.bfloat16

ascent_rate = 0.0015
select_cap = 0.5


def pieces(x):
    high = x.astype(BF16)
    rest = x - high.astype(F32)
    middle = rest.astype(BF16)
    low = (rest - middle.astype(F32)).astype(BF16)
    return high, middle, low


def pick(ones, x):
    width = x.shape[1]
    parts = jnp.dot(ones, jnp.concatenate(pieces(x), axis=1), preferred_element_type=F32)
    return parts[:, :width] + (parts[:, width : 2 * width] + parts[:, 2 * width :])


def inverse_of(x):
    return pltpu.reciprocal(x, approx=True)


def hits_of(ids, test_rows):
    shape = (test_rows, ids.shape[1])
    return jnp.where(ids == lax.broadcasted_iota(jnp.int32, shape, 0).astype(F32), 1.0, 0.0).astype(BF16)


def columns_of(blocks, hits):
    return [jnp.dot(piece, hits, preferred_element_type=F32) for piece in pieces(blocks.T)]


def total_of(columns):
    high, middle, low = columns
    return high + (middle + low)


def spread_columns(columns):
    width, slots = columns[0].shape
    whole = total_of(columns)
    stack = jnp.concatenate(columns, axis=1).astype(BF16)
    shape = (len(columns) * slots, 2 * width)
    slot = lax.broadcasted_iota(jnp.int32, shape, 0) % slots - lax.broadcasted_iota(jnp.int32, shape, 1) // width
    for s in range(0, slots, 2):
        if (s // 2) % SHARED == SHARED - 1:
            both = jnp.dot(stack, jnp.where(slot == s, 1.0, 0.0).astype(BF16), preferred_element_type=F32)
            yield both[:, :width]
            yield both[:, width:]
        else:
            yield whole[:, s : s + 1]
            yield whole[:, s + 1 : s + 2]


def slots_pass(columns, tiles, ratios, products, before=lambda s: None):
    for s, column in enumerate(spread_columns(columns)):
        before(s)
        tile = tiles[s]
        left = 1.0 - column * tile
        ratios[s] = tile * inverse_of(left)
        product = left[:8]
        for at in range(8, left.shape[0], 8):
            product = product * left[at : at + 8]
        products[8 * s : 8 * s + 8, :] = product


def logs_of(products):
    slots = products.shape[0] // 8
    part = lambda k: products[pl.ds(k, slots, stride=8), :]
    total = jnp.log(part(0) * part(1))
    for k in range(2, 8, 2):
        total = total + jnp.log(part(k) * part(k + 1))
    return total


def first_kernel(limit, rows, cols, blocks, tiles, weights, payload, ratios, held, slot_weights, ids, mine, near, row_lanes, col_lanes, own, products, sems, tile_sem, weight_sem):
    slots, width = held.shape[0], held.shape[1]
    small = [
        pltpu.make_async_copy(source, target, sems.at[i])
        for i, (source, target) in enumerate(((cols, near), (cols, col_lanes), (rows, row_lanes), (blocks, own)))
    ]
    for copy in small:
        copy.start()
    tile_copies = []
    chunk = slots // HALVES
    for group in range(HALVES):
        part = pl.ds(group * chunk, chunk)
        tile_copies.append(pltpu.make_async_copy(tiles.at[part], held.at[part], tile_sem.at[group]))
        tile_copies[-1].start()
    small[0].wait()
    for s in range(slots):
        pltpu.make_async_copy(weights.at[pl.ds(near[0, s], 1)], slot_weights.at[pl.ds(s, 1)], weight_sem).start()
    for copy in small[1:]:
        copy.wait()
    live = lax.broadcasted_iota(jnp.int32, (1, slots), 1) < limit[0]
    lanes = jnp.where(live, col_lanes[...], -1).astype(F32)
    payload[slots:, :] = jnp.broadcast_to(jnp.concatenate([lanes] * (width // slots), axis=1), (EXTRA, width))
    mine[...] = jnp.broadcast_to(jnp.where(live, col_lanes[...], -2).astype(F32), (width, slots)).T
    own_ids = row_lanes[...].astype(F32)
    ids[...] = jnp.broadcast_to(jnp.concatenate([own_ids] * (width // slots), axis=1), (EXTRA, width))
    columns = columns_of(own[...], hits_of(own_ids, own.shape[0]))

    def arrive(s):
        if s % chunk == 0:
            tile_copies[s // chunk].wait()

    slots_pass(columns, held, ratios, products, arrive)
    payload[:slots, :] = logs_of(products)
    pltpu.make_async_copy(weights.at[pl.ds(0, slots)], slot_weights, weight_sem).wait()
    alive = lax.broadcasted_iota(jnp.int32, (slots, width), 0) < limit[0]
    slot_weights[...] = jnp.where(alive, slot_weights[...], 0.0)


def matches(others, mine, start):
    slots, width = mine.shape
    here = mine[...]
    lanes = lax.broadcasted_iota(jnp.int32, (slots, width), 1)
    each = width // slots
    same = []
    for j in range(start, start + CHUNK, each):
        there = others[j, slots : slots + 1, :]
        for k in range(1, each):
            there = jnp.where(lanes < k * slots, there, others[j + k, slots : slots + 1, :])
        same.append(jnp.where(here == there, 1.0, 0.0))
    return jnp.concatenate(same, axis=1)


def log_survival(gathered, others, mine):
    slots, width = mine.shape
    total = jnp.zeros((slots, width), F32)
    for start in range(0, gathered.shape[0], CHUNK):
        rows = jnp.concatenate([gathered[j, :slots, :] for j in range(start, start + CHUNK)], axis=0)
        total = total + pick(matches(others, mine, start).astype(BF16), rows)
    return total


def all_rows_kernel(gathered, others, mine, out):
    out[...] = log_survival(gathered, others, mine)


def few_rows_kernel(received, places, own, logs, out):
    others = pick(places[...].astype(BF16), received[...].reshape(-1, received.shape[-1]))
    out[...] = others + pick(own[...].astype(BF16), logs[...])


def before_in(shape, slots):
    k, l = [lax.broadcasted_iota(jnp.int32, shape, d) for d in (0, 1)]
    return jnp.where((k // slots == l // slots) & (k < l), 1.0, 0.0).astype(BF16)


def plan_kernel(others, mine, payload, after, few, sent, places, own):
    del after
    slots, width = mine.shape
    tests = others.shape[0]
    every = tests * slots
    same = matches(others, mine, 0)
    owner = lax.broadcasted_iota(jnp.int32, (every, width), 0) // slots
    owners = jnp.where(owner == lax.broadcasted_iota(jnp.int32, (every, width), 1), 1.0, 0.0).astype(BF16)

    wanted = jnp.broadcast_to(jnp.max(same, axis=0, keepdims=True), (8, every))
    order = before_in((width, width), slots)
    ranks = jnp.concatenate(
        [jnp.dot(wanted[:, at : at + width].astype(BF16), order, preferred_element_type=F32) for at in range(0, every, width)],
        axis=1,
    )
    shape = (tests * FEW, every)
    place = lax.broadcasted_iota(jnp.int32, shape, 0)
    source = place // FEW
    here = (source == lax.broadcasted_iota(jnp.int32, shape, 1) // slots) & (source != lax.axis_index("tests")) & (wanted[:1] > 0.0)
    into = jnp.where(here & (ranks[:1] == (place % FEW).astype(F32)), 1.0, 0.0).astype(BF16)
    places[...] = lax.dot_general(same.astype(BF16), into, (((1,), (1,)), ((), ())), preferred_element_type=F32)
    own[...] = jnp.where(mine[...][:, :slots] == payload[slots : slots + 1, :slots], 1.0, 0.0)

    asked = jnp.dot(same.astype(BF16), owners, preferred_element_type=F32).T[:tests]
    asked = jnp.where(asked > 0.0, 1.0, 0.0)
    ranks = jnp.dot(asked.astype(BF16), before_in((slots, slots), slots), preferred_element_type=F32)
    row = lax.broadcasted_iota(jnp.int32, (FEW, slots), 0).astype(F32)
    sent[...] = jnp.concatenate(
        [jnp.where((asked[j : j + 1] > 0.0) & (ranks[j : j + 1] == row), 1.0, 0.0) for j in range(tests)], axis=0
    )

    table = jnp.concatenate([others[j, slots : slots + 1, :] for j in range(tests)], axis=0)
    there = [table[j : j + 1, :slots] for j in range(tests)]
    there = jnp.concatenate(there, axis=1)
    down = jnp.broadcast_to(table[:, None, :], (tests, width // tests, width)).reshape(width, width).T[:slots]
    lane = lax.broadcasted_iota(jnp.int32, (1, width), 1)
    most = jnp.zeros((1, width), F32)
    for i in range(tests):
        at = i * (width // tests)
        column = jnp.where(down[:, at : at + 1] < 0.0, -2.0, down[:, at : at + 1])
        met = jnp.where(column == there, 1.0, 0.0).astype(BF16)
        counts = jnp.sum(jnp.where(jnp.dot(met, owners, preferred_element_type=F32) > 0.0, 1.0, 0.0), axis=0, keepdims=True)
        most = jnp.maximum(most, jnp.where(lane == i, 0.0, counts))
    few[...] = jnp.broadcast_to(jnp.where(jnp.max(most, axis=1, keepdims=True) <= FEW, 1.0, 0.0), few.shape)


def slot_sums(survival, ratios, out):
    slots, width = survival.shape
    lanes = lax.broadcasted_iota(jnp.int32, (width, width), 1)
    ones = jnp.ones((width, width), BF16)
    total = jnp.zeros((width, width), F32)
    for s in range(slots):
        terms = ratios[s] * survival[s : s + 1, :]
        if s % 3 == 2:
            high = terms.astype(BF16)
            low = (terms - high.astype(F32)).astype(BF16)
            sums = jnp.dot(high, ones, preferred_element_type=F32) + jnp.dot(low, ones, preferred_element_type=F32)
        else:
            sums = jnp.sum(terms, axis=1, keepdims=True)
        total = jnp.where(lanes == s, sums, total)
    out[:slots, :] = total.T[:slots]


def gradient_kernel(gathered, mine, slot_weights, ratios, ids, out):
    slots = slot_weights.shape[0]
    slot_sums(slot_weights[...] * jnp.exp(log_survival(gathered, gathered, mine)), ratios, out)
    out[slots:, :] = ids[...]


def last_gradient_kernel(total, slot_weights, ratios, few, out, survival):
    survival[...] = slot_weights[...] * jnp.exp(total[...])
    slot_sums(survival[...], ratios, out)
    out[slot_weights.shape[0] :, :] = few[...]


def advance(current, gradient):
    rate = ascent_rate * gradient
    return current + (select_cap - current) * rate / (1.0 + rate)


def gradient_of(parts, ids, test_rows):
    slots = ids[0].shape[0] - EXTRA
    sums = [pick(hits_of(i[slots : slots + 1, :slots], test_rows), p[:slots, :]) for p, i in zip(parts, ids)]
    while len(sums) > 1:
        sums = [a + b for a, b in zip(sums[::2], sums[1::2])]
    return sums[0]


def next_kernel(branches, blocks, held, *refs):
    parts, refs = refs[:branches], refs[branches:]
    *sent, current, logs, ratios, out, products = refs if len(refs) == 6 else (*refs[:3], None, refs[3])
    test_rows, slots = blocks.shape[0], held.shape[0]
    current[...] = advance(blocks[...], gradient_of(parts, parts, test_rows))
    columns = columns_of(current[...], hits_of(parts[0][slots : slots + 1, :slots], test_rows))
    slots_pass(columns, held, ratios, products)
    rows = logs_of(products)
    logs[...] = rows
    if sent:
        out[...] = pick(sent[0][...].astype(BF16), rows).reshape(out.shape)


def tile_kernel(blocks, ids, survival, held, out, made, sems):
    slots = held.shape[0]
    columns = total_of(columns_of(blocks[...], hits_of(ids[:1, :slots], blocks.shape[0])))
    copies = []
    for s in range(slots):
        share = columns[:, s : s + 1]
        made[s] = survival[s : s + 1, :] * share * inverse_of(1.0 - share * held[s])
        if s % GROUP == GROUP - 1:
            part = pl.ds(s + 1 - GROUP, GROUP)
            copies.append(pltpu.make_async_copy(made.at[part], out.at[part], sems.at[s // GROUP]))
            copies[-1].start()
    for copy in copies:
        copy.wait()


def last_kernel(branches, current, *refs):
    *given, gradient, following, few = refs
    parts, ids = given[:branches], given[branches:]
    total = gradient_of(parts, ids, current.shape[0])
    gradient[...] = total
    following[...] = advance(current[...], total)
    slots = parts[0].shape[0] - EXTRA
    fewest = functools.reduce(jnp.minimum, [p[slots : slots + 1, :] for p in parts])
    few[0] = jnp.min(fewest).astype(jnp.int32)


SMEM = pl.BlockSpec(memory_space=pltpu.SMEM)
VMEM = pl.BlockSpec(memory_space=pltpu.VMEM)
HBM = pl.BlockSpec(memory_space=pltpu.HBM)
PARAMS = pltpu.CompilerParams(vmem_limit_bytes=24 << 20)


def sweep(tests, branches, few_rows, select, tiles, row_block, col_block, counts, weights):
    slots, width = tiles.shape[0], tiles.shape[1]
    blocks = select.reshape(-1, width)
    weight_rows = weights.reshape(-1, width)
    full = jax.ShapeDtypeStruct(tiles.shape, F32)
    per_slot = jax.ShapeDtypeStruct((slots, width), F32)
    labelled = jax.ShapeDtypeStruct((slots + EXTRA, width), F32)
    label = jax.ShapeDtypeStruct((EXTRA, width), F32)
    per_test = jax.ShapeDtypeStruct(blocks.shape, F32)
    lanes = pltpu.VMEM((1, slots), jnp.int32)
    products = pltpu.VMEM((8 * slots, width), F32)
    dma = pltpu.SemaphoreType.DMA
    far = lambda x: pltpu.with_memory_space_constraint(x, pltpu.HBM)

    def call(kernel, outs, ins, name, **more):
        return pl.pallas_call(
            kernel,
            out_shape=outs,
            in_specs=more.pop("in_specs", [VMEM] * len(ins)),
            out_specs=more.pop("out_specs", jax.tree.map(lambda _: VMEM, outs)),
            compiler_params=PARAMS,
            name=name,
            **more,
        )(*ins)

    def over_tests(x):
        return lax.all_to_all(jnp.broadcast_to(x[None], (tests,) + x.shape), "tests", 0, 0)

    def over_branches(x):
        return [x] + [lax.ppermute(x, "branches", [(b, b ^ k) for b in range(branches)]) for k in range(1, branches)]

    payload, ratios, held, slot_weights, ids, mine = call(
        first_kernel,
        (labelled, full, full, per_slot, label, per_slot),
        (counts, *(far(x) for x in (row_block.reshape(1, -1), col_block.reshape(1, -1), blocks, tiles, weight_rows))),
        "first_logs",
        in_specs=[SMEM] + [HBM] * 5,
        scratch_shapes=[
            pltpu.SMEM((1, slots), jnp.int32),
            lanes,
            lanes,
            pltpu.VMEM(blocks.shape, F32),
            products,
            dma((4,)),
            dma((HALVES,)),
            dma,
        ],
    )
    others = over_tests(payload)
    made = call(gradient_kernel, labelled, (others, mine, slot_weights, ratios, ids), "gradient")
    parts = over_branches(made)
    following_logs = functools.partial(next_kernel, branches)
    if few_rows:
        few, sent, places, own = call(
            plan_kernel,
            (
                label,
                jax.ShapeDtypeStruct((tests * FEW, slots), F32),
                jax.ShapeDtypeStruct((slots, tests * FEW), F32),
                jax.ShapeDtypeStruct((slots, slots), F32),
            ),
            (others, mine, payload, made),
            "plan",
        )
        current, logs, ratios, rows = call(
            following_logs,
            (per_test, per_slot, full, jax.ShapeDtypeStruct((tests, FEW, width), F32)),
            (blocks, held, *parts, sent),
            "next_logs",
            scratch_shapes=[products],
        )
        received = lax.all_to_all(rows, "tests", 0, 0)
        total = call(few_rows_kernel, per_slot, (received, places, own, logs), "few_rows")
    else:
        few = jnp.ones(label.shape, F32)
        current, logs, ratios = call(
            following_logs, (per_test, per_slot, full), (blocks, held, *parts), "next_logs", scratch_shapes=[products]
        )
        total = call(all_rows_kernel, per_slot, (over_tests(logs), others, mine), "all_rows")
    sums, survival = call(
        last_gradient_kernel, (labelled, per_slot), (total, slot_weights, ratios, few), "last_gradient"
    )
    last_parts = over_branches(sums)
    tile_grads = call(
        tile_kernel,
        full,
        (current, ids, survival, held),
        "tile_gradients",
        out_specs=HBM,
        scratch_shapes=[pltpu.VMEM(tiles.shape, F32), dma((slots // GROUP,))],
    )
    gradient, following, right = call(
        functools.partial(last_kernel, branches),
        (per_test, per_test, jax.ShapeDtypeStruct((1,), jnp.int32)),
        (current, *last_parts, *parts),
        "last_update",
        out_specs=(VMEM, VMEM, SMEM),
    )
    return right[0], gradient.reshape(-1), tile_grads, following.reshape(-1)


def body(tests, branches, *args):
    if tests != CHUNK:
        return sweep(tests, branches, False, *args)[1:]

    def again(state):
        kept, _ = lax.optimization_barrier((args, state[0]))
        _, *outs = sweep(tests, branches, False, *kept)
        return jnp.int32(1), *outs

    return lax.while_loop(lambda state: state[0] == 0, again, sweep(tests, branches, True, *args))[1:]


def solution(mesh):
    return jax.shard_map(
        functools.partial(body, mesh.shape["tests"], mesh.shape["branches"]),
        mesh=mesh,
        in_specs=(
            P("tests"),
            P(("tests", "branches"), None, None),
            P(("tests", "branches")),
            P(("tests", "branches")),
            P(("tests", "branches")),
            P("branches"),
        ),
        out_specs=(P("tests"), P(("tests", "branches"), None, None), P("tests")),
        check_vma=False,
    )
```

```python
import functools

import jax
import jax.numpy as jnp
from jax import lax
from jax.experimental import pallas as pl
from jax.experimental.pallas import tpu as pltpu
from jax.sharding import PartitionSpec as P

GROUP = 8
EXTRA = 8
CHUNK = 8
FEW = 16
HALVES = 2
SHARED = 3
F32 = jnp.float32
BF16 = jnp.bfloat16

ascent_rate = 0.0015
select_cap = 0.5


def pieces(x):
    high = x.astype(BF16)
    rest = x - high.astype(F32)
    middle = rest.astype(BF16)
    low = (rest - middle.astype(F32)).astype(BF16)
    return high, middle, low


def pick(ones, x, count=3):
    width = x.shape[1]
    parts = jnp.dot(ones, jnp.concatenate(pieces(x)[:count], axis=1), preferred_element_type=F32)
    low = parts[:, width : 2 * width]
    return parts[:, :width] + (low if count == 2 else low + parts[:, 2 * width :])


def inverse_of(x):
    return pltpu.reciprocal(x, approx=True)


def hits_of(ids, test_rows):
    shape = (test_rows, ids.shape[1])
    return jnp.where(ids == lax.broadcasted_iota(jnp.int32, shape, 0).astype(F32), 1.0, 0.0).astype(BF16)


def columns_of(blocks, hits):
    high, middle, low = [jnp.dot(piece, hits, preferred_element_type=F32) for piece in pieces(blocks.T)]
    return high + (middle + low)


def spread_columns(columns):
    width, slots = columns.shape
    stack = jnp.concatenate([piece.astype(F32) for piece in pieces(columns)], axis=1).astype(BF16)
    shape = (stack.shape[1], 2 * width)
    slot = lax.broadcasted_iota(jnp.int32, shape, 0) % slots - lax.broadcasted_iota(jnp.int32, shape, 1) // width
    for s in range(0, slots, 2):
        if (s // 2) % SHARED == SHARED - 1:
            both = jnp.dot(stack, jnp.where(slot == s, 1.0, 0.0).astype(BF16), preferred_element_type=F32)
            yield both[:, :width]
            yield both[:, width:]
        else:
            yield columns[:, s : s + 1]
            yield columns[:, s + 1 : s + 2]


def slots_pass(columns, tiles, ratios, products, before=lambda s: None):
    for s, column in enumerate(spread_columns(columns)):
        before(s)
        tile = tiles[s]
        left = 1.0 - column * tile
        ratios[s] = tile * inverse_of(left)
        product = left[:8]
        for at in range(8, left.shape[0], 8):
            product = product * left[at : at + 8]
        products[8 * s : 8 * s + 8, :] = product


def logs_of(products):
    slots = products.shape[0] // 8
    part = lambda k: products[pl.ds(k, slots, stride=8), :]
    total = jnp.log(part(0) * part(1))
    for k in range(2, 8, 2):
        total = total + jnp.log(part(k) * part(k + 1))
    return total


def first_kernel(limit, rows, cols, blocks, tiles, weights, payload, ratios, held, slot_weights, ids, mine, down, picked, near, row_lanes, col_lanes, own, products, sems, tile_sem, weight_sem):
    slots, width = held.shape[0], held.shape[1]
    small = [
        pltpu.make_async_copy(source, target, sems.at[i])
        for i, (source, target) in enumerate(((cols, near), (cols, col_lanes), (rows, row_lanes), (blocks, own)))
    ]
    for copy in small:
        copy.start()
    tile_copies = []
    chunk = slots // HALVES
    for group in range(HALVES):
        part = pl.ds(group * chunk, chunk)
        tile_copies.append(pltpu.make_async_copy(tiles.at[part], held.at[part], tile_sem.at[group]))
        tile_copies[-1].start()
    small[0].wait()
    for s in range(slots):
        pltpu.make_async_copy(weights.at[pl.ds(near[0, s], 1)], slot_weights.at[pl.ds(s, 1)], weight_sem).start()
    for copy in small[1:]:
        copy.wait()
    live = lax.broadcasted_iota(jnp.int32, (1, slots), 1) < limit[0]
    lanes = jnp.where(live, col_lanes[...], -1).astype(F32)
    payload[slots:, :] = jnp.broadcast_to(jnp.concatenate([lanes] * (width // slots), axis=1), (EXTRA, width))
    mine[...] = jnp.broadcast_to(jnp.where(live, col_lanes[...], -2).astype(F32), (width, slots)).T
    own_ids = row_lanes[...].astype(F32)
    ids[...] = jnp.broadcast_to(jnp.concatenate([own_ids] * (width // slots), axis=1), (EXTRA, width))
    down[...] = jnp.broadcast_to(own_ids, (width, slots)).T
    columns = columns_of(own[...], hits_of(own_ids, own.shape[0]))
    picked[...] = columns.T

    def arrive(s):
        if s % chunk == 0:
            tile_copies[s // chunk].wait()

    slots_pass(columns, held, ratios, products, arrive)
    payload[:slots, :] = logs_of(products)
    pltpu.make_async_copy(weights.at[pl.ds(0, slots)], slot_weights, weight_sem).wait()
    alive = lax.broadcasted_iota(jnp.int32, (slots, width), 0) < limit[0]
    slot_weights[...] = jnp.where(alive, slot_weights[...], 0.0)


def matches(others, mine, start):
    slots, width = mine.shape
    here = mine[...]
    lanes = lax.broadcasted_iota(jnp.int32, (slots, width), 1)
    each = width // slots
    same = []
    for j in range(start, start + CHUNK, each):
        there = others[j, slots : slots + 1, :]
        for k in range(1, each):
            there = jnp.where(lanes < k * slots, there, others[j + k, slots : slots + 1, :])
        same.append(jnp.where(here == there, 1.0, 0.0))
    return jnp.concatenate(same, axis=1)


def log_survival(gathered, others, mine):
    slots, width = mine.shape
    total = jnp.zeros((slots, width), F32)
    for start in range(0, gathered.shape[0], CHUNK):
        rows = jnp.concatenate([gathered[j, :slots, :] for j in range(start, start + CHUNK)], axis=0)
        total = total + pick(matches(others, mine, start).astype(BF16), rows)
    return total


def all_rows_kernel(gathered, others, mine, out):
    out[...] = log_survival(gathered, others, mine)


def few_rows_kernel(received, places, own, logs, out):
    others = pick(places[...].astype(BF16), received[...].reshape(-1, received.shape[-1]))
    out[...] = others + pick(own[...].astype(BF16), logs[...])


def before_in(shape, slots):
    k, l = [lax.broadcasted_iota(jnp.int32, shape, d) for d in (0, 1)]
    return jnp.where((k // slots == l // slots) & (k < l), 1.0, 0.0).astype(BF16)


def plan_kernel(others, mine, payload, after, few, sent, places, own):
    del after
    slots, width = mine.shape
    tests = others.shape[0]
    every = tests * slots
    same = matches(others, mine, 0)
    owner = lax.broadcasted_iota(jnp.int32, (every, width), 0) // slots
    owners = jnp.where(owner == lax.broadcasted_iota(jnp.int32, (every, width), 1), 1.0, 0.0).astype(BF16)

    wanted = jnp.broadcast_to(jnp.max(same, axis=0, keepdims=True), (8, every))
    order = before_in((width, width), slots)
    ranks = jnp.concatenate(
        [jnp.dot(wanted[:, at : at + width].astype(BF16), order, preferred_element_type=F32) for at in range(0, every, width)],
        axis=1,
    )
    shape = (tests * FEW, every)
    place = lax.broadcasted_iota(jnp.int32, shape, 0)
    source = place // FEW
    here = (source == lax.broadcasted_iota(jnp.int32, shape, 1) // slots) & (source != lax.axis_index("tests")) & (wanted[:1] > 0.0)
    into = jnp.where(here & (ranks[:1] == (place % FEW).astype(F32)), 1.0, 0.0).astype(BF16)
    places[...] = lax.dot_general(same.astype(BF16), into, (((1,), (1,)), ((), ())), preferred_element_type=F32)
    own[...] = jnp.where(mine[...][:, :slots] == payload[slots : slots + 1, :slots], 1.0, 0.0)

    asked = jnp.dot(same.astype(BF16), owners, preferred_element_type=F32).T[:tests]
    asked = jnp.where(asked > 0.0, 1.0, 0.0)
    ranks = jnp.dot(asked.astype(BF16), before_in((slots, slots), slots), preferred_element_type=F32)
    row = lax.broadcasted_iota(jnp.int32, (FEW, slots), 0).astype(F32)
    sent[...] = jnp.concatenate(
        [jnp.where((asked[j : j + 1] > 0.0) & (ranks[j : j + 1] == row), 1.0, 0.0) for j in range(tests)], axis=0
    )

    table = jnp.concatenate([others[j, slots : slots + 1, :] for j in range(tests)], axis=0)
    there = [table[j : j + 1, :slots] for j in range(tests)]
    there = jnp.concatenate(there, axis=1)
    down = jnp.broadcast_to(table[:, None, :], (tests, width // tests, width)).reshape(width, width).T[:slots]
    lane = lax.broadcasted_iota(jnp.int32, (1, width), 1)
    most = jnp.zeros((1, width), F32)
    for i in range(tests):
        at = i * (width // tests)
        column = jnp.where(down[:, at : at + 1] < 0.0, -2.0, down[:, at : at + 1])
        met = jnp.where(column == there, 1.0, 0.0).astype(BF16)
        counts = jnp.sum(jnp.where(jnp.dot(met, owners, preferred_element_type=F32) > 0.0, 1.0, 0.0), axis=0, keepdims=True)
        most = jnp.maximum(most, jnp.where(lane == i, 0.0, counts))
    few[...] = jnp.broadcast_to(jnp.where(jnp.max(most, axis=1, keepdims=True) <= FEW, 1.0, 0.0), few.shape)


def slot_sums(survival, ratios, out):
    slots, width = survival.shape
    lanes = lax.broadcasted_iota(jnp.int32, (width, width), 1)
    ones = jnp.ones((width, width), BF16)
    total = jnp.zeros((width, width), F32)
    for s in range(slots):
        terms = ratios[s] * survival[s : s + 1, :]
        if s % 3 == 2:
            high = terms.astype(BF16)
            low = (terms - high.astype(F32)).astype(BF16)
            sums = jnp.dot(high, ones, preferred_element_type=F32) + jnp.dot(low, ones, preferred_element_type=F32)
        else:
            sums = jnp.sum(terms, axis=1, keepdims=True)
        total = jnp.where(lanes == s, sums, total)
    out[:slots, :] = total.T[:slots]


def gradient_kernel(gathered, mine, slot_weights, ratios, ids, out):
    slots = slot_weights.shape[0]
    slot_sums(slot_weights[...] * jnp.exp(log_survival(gathered, gathered, mine)), ratios, out)
    out[slots:, :] = ids[...]


def last_gradient_kernel(total, slot_weights, ratios, few, out, survival):
    survival[...] = slot_weights[...] * jnp.exp(total[...])
    slot_sums(survival[...], ratios, out)
    out[slot_weights.shape[0] :, :] = few[...]


def advance(current, gradient):
    rate = ascent_rate * gradient
    return current + (select_cap - current) * rate / (1.0 + rate)


def in_turn(refs):
    me = lax.axis_index("branches")
    return [(me ^ k, ref) for k, ref in enumerate(refs)]


def lanes_of(rows, slots):
    width = rows[0].shape[1]
    each = width // slots
    lane = lax.broadcasted_iota(jnp.int32, (1, width), 1)
    joined = []
    for start in range(0, len(rows), each):
        row = rows[start]
        for k in range(1, each):
            row = jnp.where(lane < k * slots, row, rows[start + k])
        joined.append(row)
    return jnp.concatenate(joined, axis=1)


def next_kernel(branches, held, down, picked, *refs):
    parts, refs = refs[:branches][::-1], refs[branches:]
    *sent, columns, logs, ratios, out, products = refs if len(refs) == 6 else (*refs[:3], None, refs[3])
    slots = held.shape[0]
    ids = lanes_of([p[slots : slots + 1, :] for p in parts], slots)
    same = jnp.concatenate([down[...]] * (ids.shape[1] // down.shape[1]), axis=1) == ids
    gradient = pick(jnp.where(same, 1.0, 0.0).astype(BF16), jnp.concatenate([p[:slots, :] for p in parts], axis=0), 2)
    now = advance(picked[...], gradient).T
    columns[...] = now
    slots_pass(now, held, ratios, products)
    rows = logs_of(products)
    logs[...] = rows
    if sent:
        out[...] = pick(sent[0][...].astype(BF16), rows).reshape(out.shape)


def tile_kernel(blocks, columns, survival, held, *refs):
    *parts, out, current, hits, made, table, rows, sems = refs
    slots, width = survival.shape
    for place, part in in_turn(parts):
        table[pl.ds(place, 1), :] = part[slots : slots + 1, :]
        rows[place] = part[:slots, :]
    now = columns[...]
    copies = []
    for s in range(slots):
        share = now[:, s : s + 1]
        made[s] = survival[s : s + 1, :] * share * inverse_of(1.0 - share * held[s])
        if s % GROUP == GROUP - 1:
            group = pl.ds(s + 1 - GROUP, GROUP)
            copies.append(pltpu.make_async_copy(made.at[group], out.at[group], sems.at[s // GROUP]))
            copies[-1].start()
    ids = lanes_of([table[k : k + 1, :] for k in range(len(parts))], slots)
    every = hits_of(ids, blocks.shape[0])
    hits[...] = every.astype(F32)
    gradient = pick(every, rows[...].reshape(-1, width), 2)
    current[...] = advance(blocks[...], gradient)
    for copy in copies:
        copy.wait()


def last_kernel(current, hits, *refs):
    *given, gradient, following, few, rows = refs
    first, second, *others = given
    parts = [first, second, *others[::-1]]
    slots = rows.shape[1]
    for place, part in in_turn(parts):
        rows[place] = part[:slots, :]
    total = pick(hits[...].astype(BF16), rows[...].reshape(-1, rows.shape[2]), 2)
    gradient[...] = total
    following[...] = advance(current[...], total)
    fewest = functools.reduce(jnp.minimum, [p[slots : slots + 1, :] for p in parts])
    few[0] = jnp.min(fewest).astype(jnp.int32)


SMEM = pl.BlockSpec(memory_space=pltpu.SMEM)
VMEM = pl.BlockSpec(memory_space=pltpu.VMEM)
HBM = pl.BlockSpec(memory_space=pltpu.HBM)
PARAMS = pltpu.CompilerParams(vmem_limit_bytes=24 << 20)


def sweep(tests, branches, few_rows, select, tiles, row_block, col_block, counts, weights):
    slots, width = tiles.shape[0], tiles.shape[1]
    blocks = select.reshape(-1, width)
    weight_rows = weights.reshape(-1, width)
    full = jax.ShapeDtypeStruct(tiles.shape, F32)
    per_slot = jax.ShapeDtypeStruct((slots, width), F32)
    labelled = jax.ShapeDtypeStruct((slots + EXTRA, width), F32)
    label = jax.ShapeDtypeStruct((EXTRA, width), F32)
    per_test = jax.ShapeDtypeStruct(blocks.shape, F32)
    per_column = jax.ShapeDtypeStruct((width, slots), F32)
    lanes = pltpu.VMEM((1, slots), jnp.int32)
    products = pltpu.VMEM((8 * slots, width), F32)
    dma = pltpu.SemaphoreType.DMA
    far = lambda x: pltpu.with_memory_space_constraint(x, pltpu.HBM)

    def call(kernel, outs, ins, name, **more):
        return pl.pallas_call(
            kernel,
            out_shape=outs,
            in_specs=more.pop("in_specs", [VMEM] * len(ins)),
            out_specs=more.pop("out_specs", jax.tree.map(lambda _: VMEM, outs)),
            compiler_params=PARAMS,
            name=name,
            **more,
        )(*ins)

    def over_tests(x):
        return lax.all_to_all(jnp.broadcast_to(x[None], (tests,) + x.shape), "tests", 0, 0)

    def over_branches(x):
        return [x] + [lax.ppermute(x, "branches", [(b, b ^ k) for b in range(branches)]) for k in range(1, branches)]

    payload, ratios, held, slot_weights, ids, mine, down, picked = call(
        first_kernel,
        (labelled, full, full, per_slot, label, per_slot, per_slot, per_slot),
        (counts, *(far(x) for x in (row_block.reshape(1, -1), col_block.reshape(1, -1), blocks, tiles, weight_rows))),
        "first_logs",
        in_specs=[SMEM] + [HBM] * 5,
        scratch_shapes=[
            pltpu.SMEM((1, slots), jnp.int32),
            lanes,
            lanes,
            pltpu.VMEM(blocks.shape, F32),
            products,
            dma((4,)),
            dma((HALVES,)),
            dma,
        ],
    )
    others = over_tests(payload)
    made = call(gradient_kernel, labelled, (others, mine, slot_weights, ratios, ids), "gradient")
    parts = over_branches(made)
    following_logs = functools.partial(next_kernel, branches)
    if few_rows:
        few, sent, places, own = call(
            plan_kernel,
            (
                label,
                jax.ShapeDtypeStruct((tests * FEW, slots), F32),
                jax.ShapeDtypeStruct((slots, tests * FEW), F32),
                jax.ShapeDtypeStruct((slots, slots), F32),
            ),
            (others, mine, payload, made),
            "plan",
        )
        columns, logs, ratios, rows = call(
            following_logs,
            (per_column, per_slot, full, jax.ShapeDtypeStruct((tests, FEW, width), F32)),
            (held, down, picked, *parts[::-1], sent),
            "next_logs",
            scratch_shapes=[products],
        )
        received = lax.all_to_all(rows, "tests", 0, 0)
        total = call(few_rows_kernel, per_slot, (received, places, own, logs), "few_rows")
    else:
        few = jnp.ones(label.shape, F32)
        columns, logs, ratios = call(
            following_logs,
            (per_column, per_slot, full),
            (held, down, picked, *parts[::-1]),
            "next_logs",
            scratch_shapes=[products],
        )
        total = call(all_rows_kernel, per_slot, (over_tests(logs), others, mine), "all_rows")
    sums, survival = call(
        last_gradient_kernel, (labelled, per_slot), (total, slot_weights, ratios, few), "last_gradient"
    )
    last_parts = over_branches(sums)
    part_rows = pltpu.VMEM((branches, slots, width), F32)
    tile_grads, current, hits = call(
        tile_kernel,
        (full, per_test, jax.ShapeDtypeStruct((blocks.shape[0], branches * slots), F32)),
        (blocks, columns, survival, held, *parts),
        "tile_gradients",
        out_specs=(HBM, VMEM, VMEM),
        scratch_shapes=[
            pltpu.VMEM(tiles.shape, F32),
            pltpu.VMEM((8, width), F32),
            part_rows,
            dma((slots // GROUP,)),
        ],
    )
    gradient, following, right = call(
        last_kernel,
        (per_test, per_test, jax.ShapeDtypeStruct((1,), jnp.int32)),
        (current, hits, *last_parts[:2], *last_parts[:1:-1]),
        "last_update",
        out_specs=(VMEM, VMEM, SMEM),
        scratch_shapes=[part_rows],
    )
    return right[0], gradient.reshape(-1), tile_grads, following.reshape(-1)


def body(tests, branches, *args):
    if tests != CHUNK:
        return sweep(tests, branches, False, *args)[1:]

    def again(state):
        kept, _ = lax.optimization_barrier((args, state[0]))
        _, *outs = sweep(tests, branches, False, *kept)
        return jnp.int32(1), *outs

    return lax.while_loop(lambda state: state[0] == 0, again, sweep(tests, branches, True, *args))[1:]


def solution(mesh):
    return jax.shard_map(
        functools.partial(body, mesh.shape["tests"], mesh.shape["branches"]),
        mesh=mesh,
        in_specs=(
            P("tests"),
            P(("tests", "branches"), None, None),
            P(("tests", "branches")),
            P(("tests", "branches")),
            P(("tests", "branches")),
            P("branches"),
        ),
        out_specs=(P("tests"), P(("tests", "branches"), None, None), P("tests")),
        check_vma=False,
    )
```

```python
import functools

import jax
import jax.numpy as jnp
from jax import lax
from jax.experimental import pallas as pl
from jax.experimental.pallas import tpu as pltpu
from jax.sharding import PartitionSpec as P

GROUP = 8
EXTRA = 8
CHUNK = 8
FEW = 16
HALVES = 2
SHARED = 3
F32 = jnp.float32
BF16 = jnp.bfloat16

ascent_rate = 0.0015
select_cap = 0.5


def pieces(x):
    high = x.astype(BF16)
    rest = x - high.astype(F32)
    middle = rest.astype(BF16)
    low = (rest - middle.astype(F32)).astype(BF16)
    return high, middle, low


def pick(ones, x, count=3):
    width = x.shape[1]
    parts = jnp.dot(ones, jnp.concatenate(pieces(x)[:count], axis=1), preferred_element_type=F32)
    low = parts[:, width : 2 * width]
    return parts[:, :width] + (low if count == 2 else low + parts[:, 2 * width :])


def inverse_of(x):
    return pltpu.reciprocal(x, approx=True)


def hits_of(ids, test_rows):
    shape = (test_rows, ids.shape[1])
    return jnp.where(ids == lax.broadcasted_iota(jnp.int32, shape, 0).astype(F32), 1.0, 0.0).astype(BF16)


def columns_of(blocks, hits):
    high, middle, low = [jnp.dot(piece, hits, preferred_element_type=F32) for piece in pieces(blocks.T)]
    return high + (middle + low)


def spread_columns(columns):
    width, slots = columns.shape
    stack = jnp.concatenate([piece.astype(F32) for piece in pieces(columns)], axis=1).astype(BF16)
    shape = (stack.shape[1], 2 * width)
    slot = lax.broadcasted_iota(jnp.int32, shape, 0) % slots - lax.broadcasted_iota(jnp.int32, shape, 1) // width
    for s in range(0, slots, 2):
        if (s // 2) % SHARED == SHARED - 1:
            both = jnp.dot(stack, jnp.where(slot == s, 1.0, 0.0).astype(BF16), preferred_element_type=F32)
            yield both[:, :width]
            yield both[:, width:]
        else:
            yield columns[:, s : s + 1]
            yield columns[:, s + 1 : s + 2]


def slots_pass(columns, tiles, ratios, products, before=lambda s: None):
    for s, column in enumerate(spread_columns(columns)):
        before(s)
        tile = tiles[s]
        left = 1.0 - column * tile
        ratios[s] = tile * inverse_of(left)
        product = left[:8]
        for at in range(8, left.shape[0], 8):
            product = product * left[at : at + 8]
        products[8 * s : 8 * s + 8, :] = product


def logs_of(products):
    slots = products.shape[0] // 8
    part = lambda k: products[pl.ds(k, slots, stride=8), :]
    total = jnp.log(part(0) * part(1))
    for k in range(2, 8, 2):
        total = total + jnp.log(part(k) * part(k + 1))
    return total


def first_kernel(limit, rows, cols, blocks, tiles, weights, payload, ratios, held, slot_weights, ids, mine, down, picked, near, row_lanes, col_lanes, own, products, sems, tile_sem, weight_sem):
    slots, width = held.shape[0], held.shape[1]
    small = [
        pltpu.make_async_copy(source, target, sems.at[i])
        for i, (source, target) in enumerate(((cols, near), (cols, col_lanes), (rows, row_lanes), (blocks, own)))
    ]
    for copy in small:
        copy.start()
    tile_copies = []
    chunk = slots // HALVES
    for group in range(HALVES):
        part = pl.ds(group * chunk, chunk)
        tile_copies.append(pltpu.make_async_copy(tiles.at[part], held.at[part], tile_sem.at[group]))
        tile_copies[-1].start()
    small[0].wait()
    for s in range(slots):
        pltpu.make_async_copy(weights.at[pl.ds(near[0, s], 1)], slot_weights.at[pl.ds(s, 1)], weight_sem).start()
    for copy in small[1:]:
        copy.wait()
    live = lax.broadcasted_iota(jnp.int32, (1, slots), 1) < limit[0]
    lanes = jnp.where(live, col_lanes[...], -1).astype(F32)
    payload[slots:, :] = jnp.broadcast_to(jnp.concatenate([lanes] * (width // slots), axis=1), (EXTRA, width))
    mine[...] = jnp.broadcast_to(jnp.where(live, col_lanes[...], -2).astype(F32), (width, slots)).T
    own_ids = row_lanes[...].astype(F32)
    ids[...] = jnp.broadcast_to(jnp.concatenate([own_ids] * (width // slots), axis=1), (EXTRA, width))
    down[...] = jnp.broadcast_to(own_ids, (width, slots)).T
    columns = columns_of(own[...], hits_of(own_ids, own.shape[0]))
    picked[...] = columns.T

    def arrive(s):
        if s % chunk == 0:
            tile_copies[s // chunk].wait()

    slots_pass(columns, held, ratios, products, arrive)
    payload[:slots, :] = logs_of(products)
    pltpu.make_async_copy(weights.at[pl.ds(0, slots)], slot_weights, weight_sem).wait()
    alive = lax.broadcasted_iota(jnp.int32, (slots, width), 0) < limit[0]
    slot_weights[...] = jnp.where(alive, slot_weights[...], 0.0)


def matches(others, mine, start):
    slots, width = mine.shape
    here = mine[...]
    lanes = lax.broadcasted_iota(jnp.int32, (slots, width), 1)
    each = width // slots
    same = []
    for j in range(start, start + CHUNK, each):
        there = others[j, slots : slots + 1, :]
        for k in range(1, each):
            there = jnp.where(lanes < k * slots, there, others[j + k, slots : slots + 1, :])
        same.append(jnp.where(here == there, 1.0, 0.0))
    return jnp.concatenate(same, axis=1)


def log_survival(gathered, others, mine):
    slots, width = mine.shape
    total = jnp.zeros((slots, width), F32)
    for start in range(0, gathered.shape[0], CHUNK):
        rows = jnp.concatenate([gathered[j, :slots, :] for j in range(start, start + CHUNK)], axis=0)
        total = total + pick(matches(others, mine, start).astype(BF16), rows)
    return total


def all_rows_kernel(gathered, others, mine, out):
    out[...] = log_survival(gathered, others, mine)


def few_rows_kernel(received, places, own, logs, out):
    others = pick(places[...].astype(BF16), received[...].reshape(-1, received.shape[-1]))
    out[...] = others + pick(own[...].astype(BF16), logs[...])


def before_in(shape, slots):
    k, l = [lax.broadcasted_iota(jnp.int32, shape, d) for d in (0, 1)]
    return jnp.where((k // slots == l // slots) & (k < l), 1.0, 0.0).astype(BF16)


def plan_kernel(others, mine, payload, after, few, sent, places, own):
    del after
    slots, width = mine.shape
    tests = others.shape[0]
    every = tests * slots
    same = matches(others, mine, 0)
    owner = lax.broadcasted_iota(jnp.int32, (every, width), 0) // slots
    owners = jnp.where(owner == lax.broadcasted_iota(jnp.int32, (every, width), 1), 1.0, 0.0).astype(BF16)

    wanted = jnp.broadcast_to(jnp.max(same, axis=0, keepdims=True), (8, every))
    order = before_in((width, width), slots)
    ranks = jnp.concatenate(
        [jnp.dot(wanted[:, at : at + width].astype(BF16), order, preferred_element_type=F32) for at in range(0, every, width)],
        axis=1,
    )
    shape = (tests * FEW, every)
    place = lax.broadcasted_iota(jnp.int32, shape, 0)
    source = place // FEW
    here = (source == lax.broadcasted_iota(jnp.int32, shape, 1) // slots) & (source != lax.axis_index("tests")) & (wanted[:1] > 0.0)
    into = jnp.where(here & (ranks[:1] == (place % FEW).astype(F32)), 1.0, 0.0).astype(BF16)
    places[...] = lax.dot_general(same.astype(BF16), into, (((1,), (1,)), ((), ())), preferred_element_type=F32)
    own[...] = jnp.where(mine[...][:, :slots] == payload[slots : slots + 1, :slots], 1.0, 0.0)

    asked = jnp.dot(same.astype(BF16), owners, preferred_element_type=F32).T[:tests]
    asked = jnp.where(asked > 0.0, 1.0, 0.0)
    ranks = jnp.dot(asked.astype(BF16), before_in((slots, slots), slots), preferred_element_type=F32)
    row = lax.broadcasted_iota(jnp.int32, (FEW, slots), 0).astype(F32)
    sent[...] = jnp.concatenate(
        [jnp.where((asked[j : j + 1] > 0.0) & (ranks[j : j + 1] == row), 1.0, 0.0) for j in range(tests)], axis=0
    )

    table = jnp.concatenate([others[j, slots : slots + 1, :] for j in range(tests)], axis=0)
    there = [table[j : j + 1, :slots] for j in range(tests)]
    there = jnp.concatenate(there, axis=1)
    down = jnp.broadcast_to(table[:, None, :], (tests, width // tests, width)).reshape(width, width).T[:slots]
    lane = lax.broadcasted_iota(jnp.int32, (1, width), 1)
    most = jnp.zeros((1, width), F32)
    for i in range(tests):
        at = i * (width // tests)
        column = jnp.where(down[:, at : at + 1] < 0.0, -2.0, down[:, at : at + 1])
        met = jnp.where(column == there, 1.0, 0.0).astype(BF16)
        counts = jnp.sum(jnp.where(jnp.dot(met, owners, preferred_element_type=F32) > 0.0, 1.0, 0.0), axis=0, keepdims=True)
        most = jnp.maximum(most, jnp.where(lane == i, 0.0, counts))
    few[...] = jnp.broadcast_to(jnp.where(jnp.max(most, axis=1, keepdims=True) <= FEW, 1.0, 0.0), few.shape)


def slot_sums(survival, ratios, out):
    slots, width = survival.shape
    lanes = lax.broadcasted_iota(jnp.int32, (width, width), 1)
    ones = jnp.ones((width, width), BF16)
    total = jnp.zeros((width, width), F32)
    for s in range(slots):
        terms = ratios[s] * survival[s : s + 1, :]
        if s % 3 == 2:
            high = terms.astype(BF16)
            low = (terms - high.astype(F32)).astype(BF16)
            sums = jnp.dot(high, ones, preferred_element_type=F32) + jnp.dot(low, ones, preferred_element_type=F32)
        else:
            sums = jnp.sum(terms, axis=1, keepdims=True)
        total = jnp.where(lanes == s, sums, total)
    out[:slots, :] = total.T[:slots]


def gradient_kernel(gathered, mine, slot_weights, ratios, ids, out):
    slots = slot_weights.shape[0]
    slot_sums(slot_weights[...] * jnp.exp(log_survival(gathered, gathered, mine)), ratios, out)
    out[slots:, :] = ids[...]


def last_gradient_kernel(total, slot_weights, ratios, few, out, survival):
    survival[...] = slot_weights[...] * jnp.exp(total[...])
    slot_sums(survival[...], ratios, out)
    out[slot_weights.shape[0] :, :] = few[...]


def advance(current, gradient):
    rate = ascent_rate * gradient
    return current + (select_cap - current) * rate / (1.0 + rate)


def in_turn(refs):
    me = lax.axis_index("branches")
    return [(me ^ k, ref) for k, ref in enumerate(refs)]


def lanes_of(rows, slots):
    width = rows[0].shape[1]
    each = width // slots
    lane = lax.broadcasted_iota(jnp.int32, (1, width), 1)
    joined = []
    for start in range(0, len(rows), each):
        row = rows[start]
        for k in range(1, each):
            row = jnp.where(lane < k * slots, row, rows[start + k])
        joined.append(row)
    return jnp.concatenate(joined, axis=1)


def next_kernel(branches, held, down, picked, *refs):
    parts, refs = refs[:branches][::-1], refs[branches:]
    *sent, columns, logs, ratios, out, products = refs if len(refs) == 6 else (*refs[:3], None, refs[3])
    slots = held.shape[0]
    ids = lanes_of([p[slots : slots + 1, :] for p in parts], slots)
    same = jnp.concatenate([down[...]] * (ids.shape[1] // down.shape[1]), axis=1) == ids
    gradient = pick(jnp.where(same, 1.0, 0.0).astype(BF16), jnp.concatenate([p[:slots, :] for p in parts], axis=0), 2)
    now = advance(picked[...], gradient).T
    columns[...] = now
    slots_pass(now, held, ratios, products)
    rows = logs_of(products)
    logs[...] = rows
    if sent:
        out[...] = pick(sent[0][...].astype(BF16), rows).reshape(out.shape)


def tile_kernel(blocks, columns, survival, held, *refs):
    *parts, out, current, hits, made, table, rows, sems = refs
    slots, width = survival.shape
    for place, part in in_turn(parts):
        table[pl.ds(place, 1), :] = part[slots : slots + 1, :]
        rows[place] = part[:slots, :]
    now = columns[...]
    copies = []
    for s in range(slots):
        share = now[:, s : s + 1]
        made[s] = survival[s : s + 1, :] * share * inverse_of(1.0 - share * held[s])
        if s % GROUP == GROUP - 1:
            group = pl.ds(s + 1 - GROUP, GROUP)
            copies.append(pltpu.make_async_copy(made.at[group], out.at[group], sems.at[s // GROUP]))
            copies[-1].start()
    ids = lanes_of([table[k : k + 1, :] for k in range(len(parts))], slots)
    every = hits_of(ids, blocks.shape[0])
    hits[...] = every.astype(F32)
    gradient = pick(every, rows[...].reshape(-1, width), 2)
    current[...] = advance(blocks[...], gradient)
    for copy in copies:
        copy.wait()


def last_kernel(current, hits, *refs):
    *given, gradient, following, few, rows = refs
    first, second, *others = given
    parts = [first, second, *others[::-1]]
    slots = rows.shape[1]
    for place, part in in_turn(parts):
        rows[place] = part[:slots, :]
    total = pick(hits[...].astype(BF16), rows[...].reshape(-1, rows.shape[2]), 2)
    gradient[...] = total
    following[...] = advance(current[...], total)
    fewest = functools.reduce(jnp.minimum, [p[slots : slots + 1, :] for p in parts])
    few[0] = jnp.min(fewest).astype(jnp.int32)


SMEM = pl.BlockSpec(memory_space=pltpu.SMEM)
VMEM = pl.BlockSpec(memory_space=pltpu.VMEM)
HBM = pl.BlockSpec(memory_space=pltpu.HBM)
PARAMS = pltpu.CompilerParams(vmem_limit_bytes=24 << 20)


def sweep(tests, branches, few_rows, select, tiles, row_block, col_block, counts, weights):
    slots, width = tiles.shape[0], tiles.shape[1]
    blocks = select.reshape(-1, width)
    weight_rows = weights.reshape(-1, width)
    full = jax.ShapeDtypeStruct(tiles.shape, F32)
    per_slot = jax.ShapeDtypeStruct((slots, width), F32)
    labelled = jax.ShapeDtypeStruct((slots + EXTRA, width), F32)
    label = jax.ShapeDtypeStruct((EXTRA, width), F32)
    per_test = jax.ShapeDtypeStruct(blocks.shape, F32)
    per_column = jax.ShapeDtypeStruct((width, slots), F32)
    lanes = pltpu.VMEM((1, slots), jnp.int32)
    products = pltpu.VMEM((8 * slots, width), F32)
    dma = pltpu.SemaphoreType.DMA
    far = lambda x: pltpu.with_memory_space_constraint(x, pltpu.HBM)

    def call(kernel, outs, ins, name, **more):
        return pl.pallas_call(
            kernel,
            out_shape=outs,
            in_specs=more.pop("in_specs", [VMEM] * len(ins)),
            out_specs=more.pop("out_specs", jax.tree.map(lambda _: VMEM, outs)),
            compiler_params=PARAMS,
            name=name,
            **more,
        )(*ins)

    def over_tests(x):
        return lax.all_to_all(jnp.broadcast_to(x[None], (tests,) + x.shape), "tests", 0, 0)

    def over_branches(x):
        return [x] + [lax.ppermute(x, "branches", [(b, b ^ k) for b in range(branches)]) for k in range(1, branches)]

    payload, ratios, held, slot_weights, ids, mine, down, picked = call(
        first_kernel,
        (labelled, full, full, per_slot, label, per_slot, per_slot, per_slot),
        (counts, *(far(x) for x in (row_block.reshape(1, -1), col_block.reshape(1, -1), blocks, tiles, weight_rows))),
        "first_logs",
        in_specs=[SMEM] + [HBM] * 5,
        scratch_shapes=[
            pltpu.SMEM((1, slots), jnp.int32),
            lanes,
            lanes,
            pltpu.VMEM(blocks.shape, F32),
            products,
            dma((4,)),
            dma((HALVES,)),
            dma,
        ],
    )
    others = over_tests(payload)
    made = call(gradient_kernel, labelled, (others, mine, slot_weights, ratios, ids), "gradient")
    parts = over_branches(made)
    following_logs = functools.partial(next_kernel, branches)
    if few_rows:
        few, sent, places, own = call(
            plan_kernel,
            (
                label,
                jax.ShapeDtypeStruct((tests * FEW, slots), F32),
                jax.ShapeDtypeStruct((slots, tests * FEW), F32),
                jax.ShapeDtypeStruct((slots, slots), F32),
            ),
            (others, mine, payload, made),
            "plan",
        )
        columns, logs, ratios, rows = call(
            following_logs,
            (per_column, per_slot, full, jax.ShapeDtypeStruct((tests, FEW, width), F32)),
            (held, down, picked, *parts[::-1], sent),
            "next_logs",
            scratch_shapes=[products],
        )
        received = lax.all_to_all(rows, "tests", 0, 0)
        total = call(few_rows_kernel, per_slot, (received, places, own, logs), "few_rows")
    else:
        few = jnp.ones(label.shape, F32)
        columns, logs, ratios = call(
            following_logs,
            (per_column, per_slot, full),
            (held, down, picked, *parts[::-1]),
            "next_logs",
            scratch_shapes=[products],
        )
        total = call(all_rows_kernel, per_slot, (over_tests(logs), others, mine), "all_rows")
    sums, survival = call(
        last_gradient_kernel, (labelled, per_slot), (total, slot_weights, ratios, few), "last_gradient"
    )
    last_parts = over_branches(sums)
    part_rows = pltpu.VMEM((branches, slots, width), F32)
    tile_grads, current, hits = call(
        tile_kernel,
        (full, per_test, jax.ShapeDtypeStruct((blocks.shape[0], branches * slots), F32)),
        (blocks, columns, survival, held, *parts),
        "tile_gradients",
        out_specs=(HBM, VMEM, VMEM),
        scratch_shapes=[
            pltpu.VMEM(tiles.shape, F32),
            pltpu.VMEM((8, width), F32),
            part_rows,
            dma((slots // GROUP,)),
        ],
    )
    gradient, following, right = call(
        last_kernel,
        (per_test, per_test, pltpu.SMEM((1,), jnp.int32)),
        (current, hits, *last_parts[:2], *last_parts[:1:-1]),
        "last_update",
        out_specs=(VMEM, VMEM, SMEM),
        scratch_shapes=[part_rows],
    )
    return right[0], gradient.reshape(-1), tile_grads, following.reshape(-1)


def body(tests, branches, *args):
    if tests != CHUNK:
        return sweep(tests, branches, False, *args)[1:]

    def again(state):
        kept, _ = lax.optimization_barrier((args, state[0]))
        _, *outs = sweep(tests, branches, False, *kept)
        return state[0] != state[0], *outs

    right, *outs = sweep(tests, branches, True, *args)
    return lax.while_loop(lambda state: state[0], again, (right == 0, *outs))[1:]


def solution(mesh):
    return jax.shard_map(
        functools.partial(body, mesh.shape["tests"], mesh.shape["branches"]),
        mesh=mesh,
        in_specs=(
            P("tests"),
            P(("tests", "branches"), None, None),
            P(("tests", "branches")),
            P(("tests", "branches")),
            P(("tests", "branches")),
            P("branches"),
        ),
        out_specs=(P("tests"), P(("tests", "branches"), None, None), P("tests")),
        check_vma=False,
    )
```

```python
import functools

import jax
import jax.numpy as jnp
from jax import lax
from jax.experimental import pallas as pl
from jax.experimental.pallas import tpu as pltpu
from jax.sharding import PartitionSpec as P

GROUP = 8
EXTRA = 8
CHUNK = 8
FEW = 16
HALVES = 2
SHARED = 2
F32 = jnp.float32
BF16 = jnp.bfloat16

ascent_rate = 0.0015
select_cap = 0.5


def pieces(x):
    high = x.astype(BF16)
    rest = x - high.astype(F32)
    middle = rest.astype(BF16)
    low = (rest - middle.astype(F32)).astype(BF16)
    return high, middle, low


def pick(ones, x, count=3):
    width = x.shape[1]
    parts = jnp.dot(ones, jnp.concatenate(pieces(x)[:count], axis=1), preferred_element_type=F32)
    low = parts[:, width : 2 * width]
    return parts[:, :width] + (low if count == 2 else low + parts[:, 2 * width :])


def inverse_of(x):
    return pltpu.reciprocal(x, approx=True)


def hits_of(ids, test_rows):
    shape = (test_rows, ids.shape[1])
    return jnp.where(ids == lax.broadcasted_iota(jnp.int32, shape, 0).astype(F32), 1.0, 0.0).astype(BF16)


def columns_of(blocks, hits):
    high, middle, low = [jnp.dot(piece, hits, preferred_element_type=F32) for piece in pieces(blocks.T)]
    return high + (middle + low)


def spread_columns(columns):
    width, slots = columns.shape
    stack = jnp.concatenate([piece.astype(F32) for piece in pieces(columns)], axis=1).astype(BF16)
    shape = (stack.shape[1], 2 * width)
    slot = lax.broadcasted_iota(jnp.int32, shape, 0) % slots - lax.broadcasted_iota(jnp.int32, shape, 1) // width
    for s in range(0, slots, 2):
        if (s // 2) % SHARED == SHARED - 1:
            both = jnp.dot(stack, jnp.where(slot == s, 1.0, 0.0).astype(BF16), preferred_element_type=F32)
            yield both[:, :width]
            yield both[:, width:]
        else:
            yield columns[:, s : s + 1]
            yield columns[:, s + 1 : s + 2]


def slots_pass(columns, tiles, ratios, products, before=lambda s: None):
    for s, column in enumerate(spread_columns(columns)):
        before(s)
        tile = tiles[s]
        left = 1.0 - column * tile
        ratios[s] = tile * inverse_of(left)
        product = left[:8]
        for at in range(8, left.shape[0], 8):
            product = product * left[at : at + 8]
        products[8 * s : 8 * s + 8, :] = product


def logs_of(products):
    slots = products.shape[0] // 8
    part = lambda k: products[pl.ds(k, slots, stride=8), :]
    total = jnp.log(part(0) * part(1))
    for k in range(2, 8, 2):
        total = total + jnp.log(part(k) * part(k + 1))
    return total


def first_kernel(limit, rows, cols, blocks, tiles, weights, payload, ratios, held, slot_weights, ids, mine, down, picked, near, row_lanes, col_lanes, own, products, sems, tile_sem, weight_sem):
    slots, width = held.shape[0], held.shape[1]
    small = [
        pltpu.make_async_copy(source, target, sems.at[i])
        for i, (source, target) in enumerate(((cols, near), (cols, col_lanes), (rows, row_lanes), (blocks, own)))
    ]
    for copy in small:
        copy.start()
    tile_copies = []
    chunk = slots // HALVES
    for group in range(HALVES):
        part = pl.ds(group * chunk, chunk)
        tile_copies.append(pltpu.make_async_copy(tiles.at[part], held.at[part], tile_sem.at[group]))
        tile_copies[-1].start()
    small[0].wait()
    for s in range(slots):
        pltpu.make_async_copy(weights.at[pl.ds(near[0, s], 1)], slot_weights.at[pl.ds(s, 1)], weight_sem).start()
    for copy in small[1:]:
        copy.wait()
    live = lax.broadcasted_iota(jnp.int32, (1, slots), 1) < limit[0]
    lanes = jnp.where(live, col_lanes[...], -1).astype(F32)
    payload[slots:, :] = jnp.broadcast_to(jnp.concatenate([lanes] * (width // slots), axis=1), (EXTRA, width))
    mine[...] = jnp.broadcast_to(jnp.where(live, col_lanes[...], -2).astype(F32), (width, slots)).T
    own_ids = row_lanes[...].astype(F32)
    ids[...] = jnp.broadcast_to(jnp.concatenate([own_ids] * (width // slots), axis=1), (EXTRA, width))
    down[...] = jnp.broadcast_to(own_ids, (width, slots)).T
    columns = columns_of(own[...], hits_of(own_ids, own.shape[0]))
    picked[...] = columns.T

    def arrive(s):
        if s % chunk == 0:
            tile_copies[s // chunk].wait()

    slots_pass(columns, held, ratios, products, arrive)
    payload[:slots, :] = logs_of(products)
    pltpu.make_async_copy(weights.at[pl.ds(0, slots)], slot_weights, weight_sem).wait()
    alive = lax.broadcasted_iota(jnp.int32, (slots, width), 0) < limit[0]
    slot_weights[...] = jnp.where(alive, slot_weights[...], 0.0)


def matches(others, mine, start):
    slots, width = mine.shape
    here = mine[...]
    lanes = lax.broadcasted_iota(jnp.int32, (slots, width), 1)
    each = width // slots
    same = []
    for j in range(start, start + CHUNK, each):
        there = others[j, slots : slots + 1, :]
        for k in range(1, each):
            there = jnp.where(lanes < k * slots, there, others[j + k, slots : slots + 1, :])
        same.append(jnp.where(here == there, 1.0, 0.0))
    return jnp.concatenate(same, axis=1)


def log_survival(gathered, others, mine):
    slots, width = mine.shape
    total = jnp.zeros((slots, width), F32)
    for start in range(0, gathered.shape[0], CHUNK):
        rows = jnp.concatenate([gathered[j, :slots, :] for j in range(start, start + CHUNK)], axis=0)
        total = total + pick(matches(others, mine, start).astype(BF16), rows)
    return total


def all_rows_kernel(gathered, others, mine, out):
    out[...] = log_survival(gathered, others, mine)


def few_rows_kernel(received, places, own, logs, out):
    others = pick(places[...].astype(BF16), received[...].reshape(-1, received.shape[-1]))
    out[...] = others + pick(own[...].astype(BF16), logs[...])


def before_in(shape, slots):
    k, l = [lax.broadcasted_iota(jnp.int32, shape, d) for d in (0, 1)]
    return jnp.where((k // slots == l // slots) & (k < l), 1.0, 0.0).astype(BF16)


def plan_kernel(others, mine, payload, after, few, sent, places, own):
    del after
    slots, width = mine.shape
    tests = others.shape[0]
    every = tests * slots
    same = matches(others, mine, 0)
    owner = lax.broadcasted_iota(jnp.int32, (every, width), 0) // slots
    owners = jnp.where(owner == lax.broadcasted_iota(jnp.int32, (every, width), 1), 1.0, 0.0).astype(BF16)

    wanted = jnp.broadcast_to(jnp.max(same, axis=0, keepdims=True), (8, every))
    order = before_in((width, width), slots)
    ranks = jnp.concatenate(
        [jnp.dot(wanted[:, at : at + width].astype(BF16), order, preferred_element_type=F32) for at in range(0, every, width)],
        axis=1,
    )
    shape = (tests * FEW, every)
    place = lax.broadcasted_iota(jnp.int32, shape, 0)
    source = place // FEW
    here = (source == lax.broadcasted_iota(jnp.int32, shape, 1) // slots) & (source != lax.axis_index("tests")) & (wanted[:1] > 0.0)
    into = jnp.where(here & (ranks[:1] == (place % FEW).astype(F32)), 1.0, 0.0).astype(BF16)
    places[...] = lax.dot_general(same.astype(BF16), into, (((1,), (1,)), ((), ())), preferred_element_type=F32)
    own[...] = jnp.where(mine[...][:, :slots] == payload[slots : slots + 1, :slots], 1.0, 0.0)

    asked = jnp.dot(same.astype(BF16), owners, preferred_element_type=F32).T[:tests]
    asked = jnp.where(asked > 0.0, 1.0, 0.0)
    ranks = jnp.dot(asked.astype(BF16), before_in((slots, slots), slots), preferred_element_type=F32)
    row = lax.broadcasted_iota(jnp.int32, (FEW, slots), 0).astype(F32)
    sent[...] = jnp.concatenate(
        [jnp.where((asked[j : j + 1] > 0.0) & (ranks[j : j + 1] == row), 1.0, 0.0) for j in range(tests)], axis=0
    )

    table = jnp.concatenate([others[j, slots : slots + 1, :] for j in range(tests)], axis=0)
    there = [table[j : j + 1, :slots] for j in range(tests)]
    there = jnp.concatenate(there, axis=1)
    down = jnp.broadcast_to(table[:, None, :], (tests, width // tests, width)).reshape(width, width).T[:slots]
    lane = lax.broadcasted_iota(jnp.int32, (1, width), 1)
    most = jnp.zeros((1, width), F32)
    for i in range(tests):
        at = i * (width // tests)
        column = jnp.where(down[:, at : at + 1] < 0.0, -2.0, down[:, at : at + 1])
        met = jnp.where(column == there, 1.0, 0.0).astype(BF16)
        counts = jnp.sum(jnp.where(jnp.dot(met, owners, preferred_element_type=F32) > 0.0, 1.0, 0.0), axis=0, keepdims=True)
        most = jnp.maximum(most, jnp.where(lane == i, 0.0, counts))
    few[...] = jnp.broadcast_to(jnp.where(jnp.max(most, axis=1, keepdims=True) <= FEW, 1.0, 0.0), few.shape)


def slot_sums(survival, ratios, out):
    slots, width = survival.shape
    lanes = lax.broadcasted_iota(jnp.int32, (width, width), 1)
    ones = jnp.ones((width, width), BF16)
    total = jnp.zeros((width, width), F32)
    for s in range(slots):
        terms = ratios[s] * survival[s : s + 1, :]
        if s % 2 == 1:
            high = terms.astype(BF16)
            low = (terms - high.astype(F32)).astype(BF16)
            sums = jnp.dot(high, ones, preferred_element_type=F32) + jnp.dot(low, ones, preferred_element_type=F32)
        else:
            sums = jnp.sum(terms, axis=1, keepdims=True)
        total = jnp.where(lanes == s, sums, total)
    out[:slots, :] = total.T[:slots]


def gradient_kernel(gathered, mine, slot_weights, ratios, ids, out):
    slots = slot_weights.shape[0]
    slot_sums(slot_weights[...] * jnp.exp(log_survival(gathered, gathered, mine)), ratios, out)
    out[slots:, :] = ids[...]


def last_gradient_kernel(total, slot_weights, ratios, few, out, survival):
    survival[...] = slot_weights[...] * jnp.exp(total[...])
    slot_sums(survival[...], ratios, out)
    out[slot_weights.shape[0] :, :] = few[...]


def advance(current, gradient):
    rate = ascent_rate * gradient
    return current + (select_cap - current) * rate / (1.0 + rate)


def in_turn(refs):
    me = lax.axis_index("branches")
    return [(me ^ k, ref) for k, ref in enumerate(refs)]


def lanes_of(rows, slots):
    width = rows[0].shape[1]
    each = width // slots
    lane = lax.broadcasted_iota(jnp.int32, (1, width), 1)
    joined = []
    for start in range(0, len(rows), each):
        row = rows[start]
        for k in range(1, each):
            row = jnp.where(lane < k * slots, row, rows[start + k])
        joined.append(row)
    return jnp.concatenate(joined, axis=1)


def next_kernel(branches, held, down, picked, *refs):
    parts, refs = refs[:branches][::-1], refs[branches:]
    *sent, columns, logs, ratios, out, products = refs if len(refs) == 6 else (*refs[:3], None, refs[3])
    slots = held.shape[0]
    ids = lanes_of([p[slots : slots + 1, :] for p in parts], slots)
    same = jnp.concatenate([down[...]] * (ids.shape[1] // down.shape[1]), axis=1) == ids
    gradient = pick(jnp.where(same, 1.0, 0.0).astype(BF16), jnp.concatenate([p[:slots, :] for p in parts], axis=0), 2)
    now = advance(picked[...], gradient).T
    columns[...] = now
    slots_pass(now, held, ratios, products)
    rows = logs_of(products)
    logs[...] = rows
    if sent:
        out[...] = pick(sent[0][...].astype(BF16), rows).reshape(out.shape)


def tile_kernel(blocks, columns, survival, held, *refs):
    *parts, out, current, hits, made, table, rows, sems = refs
    slots, width = survival.shape
    for place, part in in_turn(parts):
        table[pl.ds(place, 1), :] = part[slots : slots + 1, :]
        rows[place] = part[:slots, :]
    now = columns[...]
    copies = []
    for s in range(slots):
        share = now[:, s : s + 1]
        made[s] = survival[s : s + 1, :] * share * inverse_of(1.0 - share * held[s])
        if s % GROUP == GROUP - 1:
            group = pl.ds(s + 1 - GROUP, GROUP)
            copies.append(pltpu.make_async_copy(made.at[group], out.at[group], sems.at[s // GROUP]))
            copies[-1].start()
    ids = lanes_of([table[k : k + 1, :] for k in range(len(parts))], slots)
    every = hits_of(ids, blocks.shape[0])
    hits[...] = every.astype(F32)
    gradient = pick(every, rows[...].reshape(-1, width), 2)
    current[...] = advance(blocks[...], gradient)
    for copy in copies:
        copy.wait()


def last_kernel(current, hits, *refs):
    *given, gradient, following, few, rows = refs
    first, second, *others = given
    parts = [first, second, *others[::-1]]
    slots = rows.shape[1]
    for place, part in in_turn(parts):
        rows[place] = part[:slots, :]
    total = pick(hits[...].astype(BF16), rows[...].reshape(-1, rows.shape[2]), 2)
    gradient[...] = total
    following[...] = advance(current[...], total)
    fewest = functools.reduce(jnp.minimum, [p[slots : slots + 1, :] for p in parts])
    few[0] = jnp.min(fewest).astype(jnp.int32)


SMEM = pl.BlockSpec(memory_space=pltpu.SMEM)
VMEM = pl.BlockSpec(memory_space=pltpu.VMEM)
HBM = pl.BlockSpec(memory_space=pltpu.HBM)
PARAMS = pltpu.CompilerParams(vmem_limit_bytes=24 << 20)


def sweep(tests, branches, few_rows, select, tiles, row_block, col_block, counts, weights):
    slots, width = tiles.shape[0], tiles.shape[1]
    blocks = select.reshape(-1, width)
    weight_rows = weights.reshape(-1, width)
    full = jax.ShapeDtypeStruct(tiles.shape, F32)
    per_slot = jax.ShapeDtypeStruct((slots, width), F32)
    labelled = jax.ShapeDtypeStruct((slots + EXTRA, width), F32)
    label = jax.ShapeDtypeStruct((EXTRA, width), F32)
    per_test = jax.ShapeDtypeStruct(blocks.shape, F32)
    per_column = jax.ShapeDtypeStruct((width, slots), F32)
    lanes = pltpu.VMEM((1, slots), jnp.int32)
    products = pltpu.VMEM((8 * slots, width), F32)
    dma = pltpu.SemaphoreType.DMA
    far = lambda x: pltpu.with_memory_space_constraint(x, pltpu.HBM)

    def call(kernel, outs, ins, name, **more):
        return pl.pallas_call(
            kernel,
            out_shape=outs,
            in_specs=more.pop("in_specs", [VMEM] * len(ins)),
            out_specs=more.pop("out_specs", jax.tree.map(lambda _: VMEM, outs)),
            compiler_params=PARAMS,
            name=name,
            **more,
        )(*ins)

    def over_tests(x):
        return lax.all_to_all(jnp.broadcast_to(x[None], (tests,) + x.shape), "tests", 0, 0)

    def over_branches(x):
        return [x] + [lax.ppermute(x, "branches", [(b, b ^ k) for b in range(branches)]) for k in range(1, branches)]

    payload, ratios, held, slot_weights, ids, mine, down, picked = call(
        first_kernel,
        (labelled, full, full, per_slot, label, per_slot, per_slot, per_slot),
        (counts, *(far(x) for x in (row_block.reshape(1, -1), col_block.reshape(1, -1), blocks, tiles, weight_rows))),
        "first_logs",
        in_specs=[SMEM] + [HBM] * 5,
        scratch_shapes=[
            pltpu.SMEM((1, slots), jnp.int32),
            lanes,
            lanes,
            pltpu.VMEM(blocks.shape, F32),
            products,
            dma((4,)),
            dma((HALVES,)),
            dma,
        ],
    )
    others = over_tests(payload)
    made = call(gradient_kernel, labelled, (others, mine, slot_weights, ratios, ids), "gradient")
    parts = over_branches(made)
    following_logs = functools.partial(next_kernel, branches)
    if few_rows:
        few, sent, places, own = call(
            plan_kernel,
            (
                label,
                jax.ShapeDtypeStruct((tests * FEW, slots), F32),
                jax.ShapeDtypeStruct((slots, tests * FEW), F32),
                jax.ShapeDtypeStruct((slots, slots), F32),
            ),
            (others, mine, payload, made),
            "plan",
        )
        columns, logs, ratios, rows = call(
            following_logs,
            (per_column, per_slot, full, jax.ShapeDtypeStruct((tests, FEW, width), F32)),
            (held, down, picked, *parts[::-1], sent),
            "next_logs",
            scratch_shapes=[products],
        )
        received = lax.all_to_all(rows, "tests", 0, 0)
        total = call(few_rows_kernel, per_slot, (received, places, own, logs), "few_rows")
    else:
        few = jnp.ones(label.shape, F32)
        columns, logs, ratios = call(
            following_logs,
            (per_column, per_slot, full),
            (held, down, picked, *parts[::-1]),
            "next_logs",
            scratch_shapes=[products],
        )
        total = call(all_rows_kernel, per_slot, (over_tests(logs), others, mine), "all_rows")
    sums, survival = call(
        last_gradient_kernel, (labelled, per_slot), (total, slot_weights, ratios, few), "last_gradient"
    )
    last_parts = over_branches(sums)
    part_rows = pltpu.VMEM((branches, slots, width), F32)
    tile_grads, current, hits = call(
        tile_kernel,
        (full, per_test, jax.ShapeDtypeStruct((blocks.shape[0], branches * slots), F32)),
        (blocks, columns, survival, held, *parts),
        "tile_gradients",
        out_specs=(HBM, VMEM, VMEM),
        scratch_shapes=[
            pltpu.VMEM(tiles.shape, F32),
            pltpu.VMEM((8, width), F32),
            part_rows,
            dma((slots // GROUP,)),
        ],
    )
    gradient, following, right = call(
        last_kernel,
        (per_test, per_test, pltpu.SMEM((1,), jnp.int32)),
        (current, hits, *last_parts[:2], *last_parts[:1:-1]),
        "last_update",
        out_specs=(VMEM, VMEM, SMEM),
        scratch_shapes=[part_rows],
    )
    return right[0], gradient.reshape(-1), tile_grads, following.reshape(-1)


def body(tests, branches, *args):
    if tests != CHUNK:
        return sweep(tests, branches, False, *args)[1:]

    def again(state):
        kept, _ = lax.optimization_barrier((args, state[0]))
        _, *outs = sweep(tests, branches, False, *kept)
        return state[0] != state[0], *outs

    right, *outs = sweep(tests, branches, True, *args)
    return lax.while_loop(lambda state: state[0], again, (right == 0, *outs))[1:]


def solution(mesh):
    return jax.shard_map(
        functools.partial(body, mesh.shape["tests"], mesh.shape["branches"]),
        mesh=mesh,
        in_specs=(
            P("tests"),
            P(("tests", "branches"), None, None),
            P(("tests", "branches")),
            P(("tests", "branches")),
            P(("tests", "branches")),
            P("branches"),
        ),
        out_specs=(P("tests"), P(("tests", "branches"), None, None), P("tests")),
        check_vma=False,
    )
```

```python
import functools

import jax
import jax.numpy as jnp
from jax import lax
from jax.experimental import pallas as pl
from jax.experimental.pallas import tpu as pltpu
from jax.sharding import PartitionSpec as P

GROUP = 8
EXTRA = 8
CHUNK = 8
FEW = 16
HALVES = 2
SHARED = 2
F32 = jnp.float32
BF16 = jnp.bfloat16

ascent_rate = 0.0015
select_cap = 0.5


def pieces(x):
    high = x.astype(BF16)
    rest = x - high.astype(F32)
    middle = rest.astype(BF16)
    low = (rest - middle.astype(F32)).astype(BF16)
    return high, middle, low


def pick(ones, x, count=3):
    width = x.shape[1]
    parts = jnp.dot(ones, jnp.concatenate(pieces(x)[:count], axis=1), preferred_element_type=F32)
    low = parts[:, width : 2 * width]
    return parts[:, :width] + (low if count == 2 else low + parts[:, 2 * width :])


def inverse_of(x):
    return pltpu.reciprocal(x, approx=True)


def hits_of(ids, test_rows):
    shape = (test_rows, ids.shape[1])
    return jnp.where(ids == lax.broadcasted_iota(jnp.int32, shape, 0).astype(F32), 1.0, 0.0).astype(BF16)


def columns_of(blocks, hits):
    high, middle, low = [jnp.dot(piece, hits, preferred_element_type=F32) for piece in pieces(blocks.T)]
    return high + (middle + low)


def spread_columns(columns):
    width, slots = columns.shape
    stack = jnp.concatenate([piece.astype(F32) for piece in pieces(columns)], axis=1).astype(BF16)
    shape = (stack.shape[1], 2 * width)
    slot = lax.broadcasted_iota(jnp.int32, shape, 0) % slots - lax.broadcasted_iota(jnp.int32, shape, 1) // width
    for s in range(0, slots, 2):
        if (s // 2) % SHARED == SHARED - 1:
            both = jnp.dot(stack, jnp.where(slot == s, 1.0, 0.0).astype(BF16), preferred_element_type=F32)
            yield both[:, :width]
            yield both[:, width:]
        else:
            yield columns[:, s : s + 1]
            yield columns[:, s + 1 : s + 2]


def slots_pass(columns, tiles, ratios, products, before=lambda s: None):
    for s, column in enumerate(spread_columns(columns)):
        before(s)
        tile = tiles[s]
        left = 1.0 - column * tile
        ratios[s] = tile * inverse_of(left)
        product = left[:8]
        for at in range(8, left.shape[0], 8):
            product = product * left[at : at + 8]
        products[8 * s : 8 * s + 8, :] = product


def logs_of(products):
    slots = products.shape[0] // 8
    part = lambda k: products[pl.ds(k, slots, stride=8), :]
    total = jnp.log(part(0) * part(1))
    for k in range(2, 8, 2):
        total = total + jnp.log(part(k) * part(k + 1))
    return total


def first_kernel(limit, rows, cols, blocks, tiles, weights, payload, ratios, held, slot_weights, ids, mine, down, picked, near, row_lanes, col_lanes, own, products, sems, tile_sem, weight_sem):
    slots, width = held.shape[0], held.shape[1]
    small = [
        pltpu.make_async_copy(source, target, sems.at[i])
        for i, (source, target) in enumerate(((cols, near), (cols, col_lanes), (rows, row_lanes), (blocks, own)))
    ]
    for copy in small:
        copy.start()
    tile_copies = []
    chunk = slots // HALVES
    for group in range(HALVES):
        part = pl.ds(group * chunk, chunk)
        tile_copies.append(pltpu.make_async_copy(tiles.at[part], held.at[part], tile_sem.at[group]))
        tile_copies[-1].start()
    small[0].wait()
    for s in range(slots):
        pltpu.make_async_copy(weights.at[pl.ds(near[0, s], 1)], slot_weights.at[pl.ds(s, 1)], weight_sem).start()
    for copy in small[1:]:
        copy.wait()
    live = lax.broadcasted_iota(jnp.int32, (1, slots), 1) < limit[0]
    lanes = jnp.where(live, col_lanes[...], -1).astype(F32)
    payload[slots:, :] = jnp.broadcast_to(jnp.concatenate([lanes] * (width // slots), axis=1), (EXTRA, width))
    mine[...] = jnp.broadcast_to(jnp.where(live, col_lanes[...], -2).astype(F32), (width, slots)).T
    own_ids = row_lanes[...].astype(F32)
    ids[...] = jnp.broadcast_to(jnp.concatenate([own_ids] * (width // slots), axis=1), (EXTRA, width))
    down[...] = jnp.broadcast_to(own_ids, (width, slots)).T
    columns = columns_of(own[...], hits_of(own_ids, own.shape[0]))
    picked[...] = columns.T

    def arrive(s):
        if s % chunk == 0:
            tile_copies[s // chunk].wait()

    slots_pass(columns, held, ratios, products, arrive)
    payload[:slots, :] = logs_of(products)
    pltpu.make_async_copy(weights.at[pl.ds(0, slots)], slot_weights, weight_sem).wait()
    alive = lax.broadcasted_iota(jnp.int32, (slots, width), 0) < limit[0]
    slot_weights[...] = jnp.where(alive, slot_weights[...], 0.0)


def matches(others, mine, start):
    slots, width = mine.shape
    here = mine[...]
    lanes = lax.broadcasted_iota(jnp.int32, (slots, width), 1)
    each = width // slots
    same = []
    for j in range(start, start + CHUNK, each):
        there = others[j, slots : slots + 1, :]
        for k in range(1, each):
            there = jnp.where(lanes < k * slots, there, others[j + k, slots : slots + 1, :])
        same.append(jnp.where(here == there, 1.0, 0.0))
    return jnp.concatenate(same, axis=1)


def log_survival(gathered, others, mine):
    slots, width = mine.shape
    total = jnp.zeros((slots, width), F32)
    for start in range(0, gathered.shape[0], CHUNK):
        rows = jnp.concatenate([gathered[j, :slots, :] for j in range(start, start + CHUNK)], axis=0)
        total = total + pick(matches(others, mine, start).astype(BF16), rows)
    return total


def all_rows_kernel(gathered, others, mine, out):
    out[...] = log_survival(gathered, others, mine)


def few_rows_kernel(received, places, own, logs, slot_weights, ratios, few, out, survival):
    rows = jnp.concatenate([received[...].reshape(-1, received.shape[-1]), logs[...]], axis=0)
    total = pick(jnp.concatenate([places[...], own[...]], axis=1).astype(BF16), rows)
    survival[...] = slot_weights[...] * jnp.exp(total)
    slot_sums(survival[...], ratios, out)
    out[slot_weights.shape[0] :, :] = few[...]


def before_in(shape, slots):
    k, l = [lax.broadcasted_iota(jnp.int32, shape, d) for d in (0, 1)]
    return jnp.where((k // slots == l // slots) & (k < l), 1.0, 0.0).astype(BF16)


def plan_kernel(others, mine, payload, after, few, sent, places, own):
    del after
    slots, width = mine.shape
    tests = others.shape[0]
    every = tests * slots
    same = matches(others, mine, 0)
    owner = lax.broadcasted_iota(jnp.int32, (every, width), 0) // slots
    owners = jnp.where(owner == lax.broadcasted_iota(jnp.int32, (every, width), 1), 1.0, 0.0).astype(BF16)

    wanted = jnp.broadcast_to(jnp.max(same, axis=0, keepdims=True), (8, every))
    order = before_in((width, width), slots)
    ranks = jnp.concatenate(
        [jnp.dot(wanted[:, at : at + width].astype(BF16), order, preferred_element_type=F32) for at in range(0, every, width)],
        axis=1,
    )
    shape = (tests * FEW, every)
    place = lax.broadcasted_iota(jnp.int32, shape, 0)
    source = place // FEW
    here = (source == lax.broadcasted_iota(jnp.int32, shape, 1) // slots) & (source != lax.axis_index("tests")) & (wanted[:1] > 0.0)
    into = jnp.where(here & (ranks[:1] == (place % FEW).astype(F32)), 1.0, 0.0).astype(BF16)
    places[...] = lax.dot_general(same.astype(BF16), into, (((1,), (1,)), ((), ())), preferred_element_type=F32)
    own[...] = jnp.where(mine[...][:, :slots] == payload[slots : slots + 1, :slots], 1.0, 0.0)

    asked = jnp.dot(same.astype(BF16), owners, preferred_element_type=F32).T[:tests]
    asked = jnp.where(asked > 0.0, 1.0, 0.0)
    ranks = jnp.dot(asked.astype(BF16), before_in((slots, slots), slots), preferred_element_type=F32)
    row = lax.broadcasted_iota(jnp.int32, (FEW, slots), 0).astype(F32)
    sent[...] = jnp.concatenate(
        [jnp.where((asked[j : j + 1] > 0.0) & (ranks[j : j + 1] == row), 1.0, 0.0) for j in range(tests)], axis=0
    )

    table = jnp.concatenate([others[j, slots : slots + 1, :] for j in range(tests)], axis=0)
    there = [table[j : j + 1, :slots] for j in range(tests)]
    there = jnp.concatenate(there, axis=1)
    down = jnp.broadcast_to(table[:, None, :], (tests, width // tests, width)).reshape(width, width).T[:slots]
    lane = lax.broadcasted_iota(jnp.int32, (1, width), 1)
    most = jnp.zeros((1, width), F32)
    for i in range(tests):
        at = i * (width // tests)
        column = jnp.where(down[:, at : at + 1] < 0.0, -2.0, down[:, at : at + 1])
        met = jnp.where(column == there, 1.0, 0.0).astype(BF16)
        counts = jnp.sum(jnp.where(jnp.dot(met, owners, preferred_element_type=F32) > 0.0, 1.0, 0.0), axis=0, keepdims=True)
        most = jnp.maximum(most, jnp.where(lane == i, 0.0, counts))
    few[...] = jnp.broadcast_to(jnp.where(jnp.max(most, axis=1, keepdims=True) <= FEW, 1.0, 0.0), few.shape)


def slot_sums(survival, ratios, out):
    slots, width = survival.shape
    lanes = lax.broadcasted_iota(jnp.int32, (width, width), 1)
    ones = jnp.ones((width, width), BF16)
    total = jnp.zeros((width, width), F32)
    for s in range(slots):
        terms = ratios[s] * survival[s : s + 1, :]
        if s % 2 == 1:
            high = terms.astype(BF16)
            low = (terms - high.astype(F32)).astype(BF16)
            sums = jnp.dot(high, ones, preferred_element_type=F32) + jnp.dot(low, ones, preferred_element_type=F32)
        else:
            sums = jnp.sum(terms, axis=1, keepdims=True)
        total = jnp.where(lanes == s, sums, total)
    out[:slots, :] = total.T[:slots]


def gradient_kernel(gathered, mine, slot_weights, ratios, ids, out):
    slots = slot_weights.shape[0]
    slot_sums(slot_weights[...] * jnp.exp(log_survival(gathered, gathered, mine)), ratios, out)
    out[slots:, :] = ids[...]


def last_gradient_kernel(total, slot_weights, ratios, few, out, survival):
    survival[...] = slot_weights[...] * jnp.exp(total[...])
    slot_sums(survival[...], ratios, out)
    out[slot_weights.shape[0] :, :] = few[...]


def advance(current, gradient):
    rate = ascent_rate * gradient
    return current + (select_cap - current) * rate / (1.0 + rate)


def in_turn(refs):
    me = lax.axis_index("branches")
    return [(me ^ k, ref) for k, ref in enumerate(refs)]


def lanes_of(rows, slots):
    width = rows[0].shape[1]
    each = width // slots
    lane = lax.broadcasted_iota(jnp.int32, (1, width), 1)
    joined = []
    for start in range(0, len(rows), each):
        row = rows[start]
        for k in range(1, each):
            row = jnp.where(lane < k * slots, row, rows[start + k])
        joined.append(row)
    return jnp.concatenate(joined, axis=1)


def next_kernel(branches, held, down, picked, *refs):
    parts, refs = refs[:branches][::-1], refs[branches:]
    *sent, columns, logs, ratios, out, products = refs if len(refs) == 6 else (*refs[:3], None, refs[3])
    slots = held.shape[0]
    ids = lanes_of([p[slots : slots + 1, :] for p in parts], slots)
    same = jnp.concatenate([down[...]] * (ids.shape[1] // down.shape[1]), axis=1) == ids
    gradient = pick(jnp.where(same, 1.0, 0.0).astype(BF16), jnp.concatenate([p[:slots, :] for p in parts], axis=0), 2)
    now = advance(picked[...], gradient).T
    columns[...] = now
    slots_pass(now, held, ratios, products)
    rows = logs_of(products)
    logs[...] = rows
    if sent:
        out[...] = pick(sent[0][...].astype(BF16), rows).reshape(out.shape)


def tile_kernel(blocks, columns, survival, held, *refs):
    *parts, out, current, hits, made, table, rows, sems = refs
    slots, width = survival.shape
    for place, part in in_turn(parts):
        table[pl.ds(place, 1), :] = part[slots : slots + 1, :]
        rows[place] = part[:slots, :]
    now = columns[...]
    copies = []
    for s in range(slots):
        share = now[:, s : s + 1]
        made[s] = survival[s : s + 1, :] * share * inverse_of(1.0 - share * held[s])
        if s % GROUP == GROUP - 1:
            group = pl.ds(s + 1 - GROUP, GROUP)
            copies.append(pltpu.make_async_copy(made.at[group], out.at[group], sems.at[s // GROUP]))
            copies[-1].start()
    ids = lanes_of([table[k : k + 1, :] for k in range(len(parts))], slots)
    every = hits_of(ids, blocks.shape[0])
    hits[...] = every.astype(F32)
    gradient = pick(every, rows[...].reshape(-1, width), 2)
    current[...] = advance(blocks[...], gradient)
    for copy in copies:
        copy.wait()


def last_kernel(current, hits, *refs):
    *given, gradient, following, few, rows = refs
    first, second, *others = given
    parts = [first, second, *others[::-1]]
    slots = rows.shape[1]
    for place, part in in_turn(parts):
        rows[place] = part[:slots, :]
    total = pick(hits[...].astype(BF16), rows[...].reshape(-1, rows.shape[2]), 2)
    gradient[...] = total
    following[...] = advance(current[...], total)
    fewest = functools.reduce(jnp.minimum, [p[slots : slots + 1, :] for p in parts])
    few[0] = jnp.min(fewest).astype(jnp.int32)


SMEM = pl.BlockSpec(memory_space=pltpu.SMEM)
VMEM = pl.BlockSpec(memory_space=pltpu.VMEM)
HBM = pl.BlockSpec(memory_space=pltpu.HBM)
PARAMS = pltpu.CompilerParams(vmem_limit_bytes=24 << 20)


def sweep(tests, branches, few_rows, select, tiles, row_block, col_block, counts, weights):
    slots, width = tiles.shape[0], tiles.shape[1]
    blocks = select.reshape(-1, width)
    weight_rows = weights.reshape(-1, width)
    full = jax.ShapeDtypeStruct(tiles.shape, F32)
    per_slot = jax.ShapeDtypeStruct((slots, width), F32)
    labelled = jax.ShapeDtypeStruct((slots + EXTRA, width), F32)
    label = jax.ShapeDtypeStruct((EXTRA, width), F32)
    per_test = jax.ShapeDtypeStruct(blocks.shape, F32)
    per_column = jax.ShapeDtypeStruct((width, slots), F32)
    lanes = pltpu.VMEM((1, slots), jnp.int32)
    products = pltpu.VMEM((8 * slots, width), F32)
    dma = pltpu.SemaphoreType.DMA
    far = lambda x: pltpu.with_memory_space_constraint(x, pltpu.HBM)

    def call(kernel, outs, ins, name, **more):
        return pl.pallas_call(
            kernel,
            out_shape=outs,
            in_specs=more.pop("in_specs", [VMEM] * len(ins)),
            out_specs=more.pop("out_specs", jax.tree.map(lambda _: VMEM, outs)),
            compiler_params=PARAMS,
            name=name,
            **more,
        )(*ins)

    def over_tests(x):
        return lax.all_to_all(jnp.broadcast_to(x[None], (tests,) + x.shape), "tests", 0, 0)

    def over_branches(x):
        return [x] + [lax.ppermute(x, "branches", [(b, b ^ k) for b in range(branches)]) for k in range(1, branches)]

    payload, ratios, held, slot_weights, ids, mine, down, picked = call(
        first_kernel,
        (labelled, full, full, per_slot, label, per_slot, per_slot, per_slot),
        (counts, *(far(x) for x in (row_block.reshape(1, -1), col_block.reshape(1, -1), blocks, tiles, weight_rows))),
        "first_logs",
        in_specs=[SMEM] + [HBM] * 5,
        scratch_shapes=[
            pltpu.SMEM((1, slots), jnp.int32),
            lanes,
            lanes,
            pltpu.VMEM(blocks.shape, F32),
            products,
            dma((4,)),
            dma((HALVES,)),
            dma,
        ],
    )
    others = over_tests(payload)
    made = call(gradient_kernel, labelled, (others, mine, slot_weights, ratios, ids), "gradient")
    parts = over_branches(made)
    following_logs = functools.partial(next_kernel, branches)
    if few_rows:
        few, sent, places, own = call(
            plan_kernel,
            (
                label,
                jax.ShapeDtypeStruct((tests * FEW, slots), F32),
                jax.ShapeDtypeStruct((slots, tests * FEW), F32),
                jax.ShapeDtypeStruct((slots, slots), F32),
            ),
            (others, mine, payload, made),
            "plan",
        )
        columns, logs, ratios, rows = call(
            following_logs,
            (per_column, per_slot, full, jax.ShapeDtypeStruct((tests, FEW, width), F32)),
            (held, down, picked, *parts[::-1], sent),
            "next_logs",
            scratch_shapes=[products],
        )
        received = lax.all_to_all(rows, "tests", 0, 0)
        sums, survival = call(
            few_rows_kernel, (labelled, per_slot), (received, places, own, logs, slot_weights, ratios, few), "last_gradient"
        )
    else:
        few = jnp.ones(label.shape, F32)
        columns, logs, ratios = call(
            following_logs,
            (per_column, per_slot, full),
            (held, down, picked, *parts[::-1]),
            "next_logs",
            scratch_shapes=[products],
        )
        total = call(all_rows_kernel, per_slot, (over_tests(logs), others, mine), "all_rows")
        sums, survival = call(
            last_gradient_kernel, (labelled, per_slot), (total, slot_weights, ratios, few), "last_gradient"
        )
    last_parts = over_branches(sums)
    part_rows = pltpu.VMEM((branches, slots, width), F32)
    tile_grads, current, hits = call(
        tile_kernel,
        (full, per_test, jax.ShapeDtypeStruct((blocks.shape[0], branches * slots), F32)),
        (blocks, columns, survival, held, *parts),
        "tile_gradients",
        out_specs=(HBM, VMEM, VMEM),
        scratch_shapes=[
            pltpu.VMEM(tiles.shape, F32),
            pltpu.VMEM((8, width), F32),
            part_rows,
            dma((slots // GROUP,)),
        ],
    )
    gradient, following, right = call(
        last_kernel,
        (per_test, per_test, pltpu.SMEM((1,), jnp.int32)),
        (current, hits, *last_parts[:2], *last_parts[:1:-1]),
        "last_update",
        out_specs=(VMEM, VMEM, SMEM),
        scratch_shapes=[part_rows],
    )
    return right[0], gradient.reshape(-1), tile_grads, following.reshape(-1)


def body(tests, branches, *args):
    if tests != CHUNK:
        return sweep(tests, branches, False, *args)[1:]

    def again(state):
        kept, _ = lax.optimization_barrier((args, state[0]))
        _, *outs = sweep(tests, branches, False, *kept)
        return state[0] != state[0], *outs

    right, *outs = sweep(tests, branches, True, *args)
    return lax.while_loop(lambda state: state[0], again, (right == 0, *outs))[1:]


def solution(mesh):
    return jax.shard_map(
        functools.partial(body, mesh.shape["tests"], mesh.shape["branches"]),
        mesh=mesh,
        in_specs=(
            P("tests"),
            P(("tests", "branches"), None, None),
            P(("tests", "branches")),
            P(("tests", "branches")),
            P(("tests", "branches")),
            P("branches"),
        ),
        out_specs=(P("tests"), P(("tests", "branches"), None, None), P("tests")),
        check_vma=False,
    )
```
